256 devices in a mesh: rows: 32 (over x, z), tp: 8 (over y, core).
Axes of the slice: x: 4, y: 4, z: 8, core: 2. Of those that a mesh axis runs over, the one named last changes fastest.
Arguments:
- text_embed: bfloat16 [24576, 8192], P('rows', 'tp'), may hold values from -24 to 24
- image_embed: bfloat16 [12288, 8192], P('rows', 'tp'), may hold values from -24 to 24
- image_start: int32 [512], replicated, may hold values from 0 to 24552, as said below
- norm_gain: float32 [8192], P('tp'), may hold values from 0.25 to 1.75
- key_weight: bfloat16 [8192, 1024], P('tp'), may hold values from -0.0625 to 0.0625
- value_weight: bfloat16 [8192, 1024], P('tp'), may hold values from -0.0625 to 0.0625
- key_target: bfloat16 [24576, 1024], P('rows', 'tp'), may hold values from -6 to 6
- value_target: bfloat16 [24576, 1024], P('rows', 'tp'), may hold values from -6 to 6
Outputs:
- keys: bfloat16 [24576, 1024], P('rows', 'tp')
- values: bfloat16 [24576, 1024], P('rows', 'tp')
- text_grad: bfloat16 [24576, 8192], P('rows', 'tp')
- image_grad: bfloat16 [12288, 8192], P('rows', 'tp')
The draws below stay inside these ranges and needn't reach their ends.
Inputs may be any that keep to these rules, and one draw needn't show every extreme that they name: `image_start`: every image lies inside one block of 768 positions (block b holds positions b * 768 .. (b + 1) * 768 - 1); images never intersect; the 16 images of one index of rows (images r * 16 .. r * 16 + 15) lie in 16 different blocks; a block holds at most 32 images, and some block holds exactly that many (it holds no text) while another holds none.
All inputs are finite; a program needn't handle non-finite values.
Results may differ from the reference program's by a relative error of at most 0.014.
Values may be sent and summed in bfloat16 or wider, within the bound.
No kernel may reach another device: no remote copies, remote signals or barrier semaphores. Data moves between devices by JAX's collectives and lax.ppermute only.
A program may use at most 64 MiB of HBM per device.

```python
import math
import jax
import jax.numpy as jnp
from jax import lax

WIDTH = 8192
IMAGES_DEV = 16
IMAGE_LEN = 24
KV_WIDTH = 1024
SEQ_DEV = 768
TOKENS = 24576
IMAGE_TOKENS = 12288
N_ROWS = 32


def rough_rows(key, count, row_low, row_high):
    first, second, third = jax.random.split(key, 3)
    column_scale = jnp.exp(jax.random.uniform(first, (WIDTH,), jnp.float32, math.log(0.3), math.log(3.0)))
    row_scale = jnp.exp(jax.random.uniform(second, (count, 1), jnp.float32, math.log(row_low), math.log(row_high)))
    base = jax.random.truncated_normal(third, -4.0, 4.0, (count, WIDTH), jnp.float32)
    return base * row_scale * column_scale[None, :]


def draw_text_embed(key, part):
    key = jax.random.fold_in(key, 11)
    values = rough_rows(key, TOKENS, 0.5, 2.0)
    return values.astype(jnp.bfloat16)


def draw_image_embed(key, part):
    key = jax.random.fold_in(key, 13)
    values = rough_rows(key, IMAGE_TOKENS, 0.5, 2.0)
    return values.astype(jnp.bfloat16)


def draw_image_start(key, part):
    key = jax.random.fold_in(key, 5)
    first, second, third = jax.random.split(key, 3)
    shards = N_ROWS
    per_dev = IMAGES_DEV
    order = jax.random.permutation(first, shards).astype(jnp.int32)
    extra = jax.random.randint(second, (shards // 2,), 0, per_dev + 1).astype(jnp.int32)
    extra = extra.at[0].set(per_dev)
    loads = jnp.stack([per_dev + extra, per_dev - extra], axis=1).reshape(shards)
    ends = jnp.cumsum(loads).astype(jnp.int32)
    slots = jnp.arange(shards * per_dev, dtype=jnp.int32)
    seq_index = jnp.sum((ends[None, :] <= slots[:, None]).astype(jnp.int32), axis=1)
    target = order[seq_index]
    rank = slots - (ends - loads)[seq_index]
    free_text = SEQ_DEV - loads * IMAGE_LEN
    cuts = jax.random.randint(third, (shards, 2 * per_dev), 0, free_text[:, None] + 1).astype(jnp.int32)
    used = jnp.arange(2 * per_dev, dtype=jnp.int32)[None, :] < loads[:, None]
    cuts = jnp.sort(jnp.where(used, cuts, 4 * SEQ_DEV), axis=1)
    start = target * SEQ_DEV + cuts[seq_index, rank] + rank * IMAGE_LEN
    return start.reshape(per_dev, shards).T.reshape(shards * per_dev).astype(jnp.int32)


def block_scale(rng, dims, cuts, least, high):
    def one(dim, blocks):
        steps = jax.random.uniform(jax.random.fold_in(jax.random.fold_in(rng, 6), dim), (blocks,), jnp.float32, least / len(cuts), high / len(cuts))
        return jnp.repeat(jnp.exp(steps), dims[dim] // blocks).reshape((-1,) + (1,) * (len(dims) - dim - 1))

    loudness = one(*cuts[0])
    for cut in cuts[1:]:
        loudness = loudness * one(*cut)
    return loudness


def bell_draw(rng, extent, deviation, reach, cuts=(), held_as=jnp.bfloat16):
    values = deviation * jax.random.normal(rng, extent, jnp.float32)
    if cuts:
        values = values * block_scale(rng, extent, cuts, -0.22, 0.18)
    return jnp.clip(values, -reach, reach).astype(held_as)


def setup_inputs(seed: int = 0) -> dict:
    key_of = jax.random.split(jax.random.key(seed), 9)
    text_embed = draw_text_embed(jax.random.fold_in(key_of[8], 71), 0)
    image_embed = draw_image_embed(jax.random.fold_in(key_of[8], 71), 0)
    image_start = draw_image_start(jax.random.fold_in(key_of[8], 71), 0)
    norm_gain = jnp.clip(1.0 + 0.15 * jax.random.normal(key_of[3], (WIDTH,), jnp.float32), 0.25, 1.75)
    key_weight = bell_draw(key_of[4], (WIDTH, KV_WIDTH), WIDTH ** -0.5, 0.0625, ((0, 8),))
    value_weight = bell_draw(key_of[5], (WIDTH, KV_WIDTH), WIDTH ** -0.5, 0.0625, ((0, 8),))
    key_target = bell_draw(key_of[6], (TOKENS, KV_WIDTH), 1.0, 6.0, ((0, 32), (1, 8)))
    value_target = bell_draw(key_of[7], (TOKENS, KV_WIDTH), 1.0, 6.0, ((0, 32), (1, 8)))
    return {"text_embed": text_embed, "image_embed": image_embed, "image_start": image_start, "norm_gain": norm_gain, "key_weight": key_weight, "value_weight": value_weight, "key_target": key_target, "value_target": value_target}


epsilon = 1e-06

def image_rows(image_start):
    within = jnp.arange(IMAGE_LEN, dtype=jnp.int32)
    return (image_start[:, None] + within[None, :]).reshape(-1).astype(jnp.int32)

def reference(text_embed, image_embed, image_start, norm_gain, key_weight, value_weight, key_target, value_target):
    positions = image_rows(image_start)
    assembled = text_embed.at[positions].set(image_embed)
    marked = jnp.zeros((TOKENS,), jnp.float32).at[positions].set(1.0)

    def one_block(pieces):
        block, key_goal, value_goal = pieces
        stream = block.astype(jnp.float32)
        squares = lax.optimization_barrier(jnp.sum(stream * stream, axis=1))
        inverse = lax.rsqrt(squares / WIDTH + epsilon)
        scaled = (norm_gain[None, :] * stream).astype(jnp.bfloat16)
        key_raw = jnp.dot(scaled, key_weight, preferred_element_type=jnp.float32)
        value_raw = jnp.dot(scaled, value_weight, preferred_element_type=jnp.float32)
        keys = (inverse[:, None] * key_raw).astype(jnp.bfloat16)
        values = (inverse[:, None] * value_raw).astype(jnp.bfloat16)
        key_resid = (keys.astype(jnp.float32) - key_goal.astype(jnp.float32)).astype(jnp.bfloat16)
        value_resid = (values.astype(jnp.float32) - value_goal.astype(jnp.float32)).astype(jnp.bfloat16)
        radial = lax.optimization_barrier(jnp.sum(key_resid.astype(jnp.float32) * keys.astype(jnp.float32) + value_resid.astype(jnp.float32) * values.astype(jnp.float32), axis=1)) / inverse
        back = jnp.dot(key_resid, key_weight.T, preferred_element_type=jnp.float32)
        back = back + jnp.dot(value_resid, value_weight.T, preferred_element_type=jnp.float32)
        grad = norm_gain[None, :] * inverse[:, None] * back - (inverse ** 3 * radial / WIDTH)[:, None] * stream
        return (keys, values, grad)
    keys, values, grads = lax.map(one_block, (assembled.reshape(N_ROWS, SEQ_DEV, WIDTH), key_target.reshape(N_ROWS, SEQ_DEV, KV_WIDTH), value_target.reshape(N_ROWS, SEQ_DEV, KV_WIDTH)))
    grads = grads.reshape(TOKENS, WIDTH)
    text_grad = jnp.where(marked[:, None] > 0.5, 0.0, grads).astype(jnp.bfloat16)
    image_grad = grads[positions].astype(jnp.bfloat16)
    return (keys.reshape(TOKENS, KV_WIDTH), values.reshape(TOKENS, KV_WIDTH), text_grad, image_grad)
```

```python
import functools

import jax
import jax.numpy as jnp
from jax import lax
from jax.experimental import pallas as pl
from jax.experimental.pallas import tpu as pltpu
from jax.sharding import PartitionSpec as P

WIDTH = 8192
EPSILON = 1e-06
IMAGE_LEN = 24
GROUP = 384
EXTRA = 16
HEAD = 128
PAIR = 2 * HEAD
RINGS = 4

F32 = jnp.float32
BF16 = jnp.bfloat16
PARAMS = pltpu.CompilerParams(vmem_limit_bytes=40 * 2**20)


def identity_mask():
    shape = (HEAD, HEAD)
    return lax.broadcasted_iota(jnp.int32, shape, 0) == lax.broadcasted_iota(jnp.int32, shape, 1)


def column_to_lanes(column):
    eye = identity_mask()
    row = lax.broadcasted_iota(jnp.int32, (8, HEAD), 0)
    out = jnp.zeros((8, HEAD), F32)
    for p in range(GROUP // HEAD):
        piece = column[p * HEAD : (p + 1) * HEAD, :]
        lanes = jnp.sum(jnp.where(eye, piece, 0.0), axis=0, keepdims=True)
        out = jnp.where(row == p, lanes, out)
    return out


def lanes_to_column(lanes):
    eye = identity_mask()
    pieces = [
        jnp.sum(jnp.where(eye, lanes[p : p + 1, :], 0.0), axis=1, keepdims=True)
        for p in range(GROUP // HEAD)
    ]
    return jnp.concatenate(pieces, axis=0)


def split_extra(lanes):
    high = lanes.astype(BF16).astype(F32)
    both = jnp.concatenate([high, lanes - high], axis=0)
    return jnp.concatenate([both, jnp.zeros((EXTRA, HEAD), F32)], axis=1).astype(BF16)


def join_extra(block):
    block = block.astype(F32)
    return block[0:8, 0:HEAD] + block[8:16, 0:HEAD]


def prepare(x_ref, gain_ref, scaled, lanes):
    x = x_ref[...].astype(F32)
    scaled[...] = (gain_ref[...] * x).astype(BF16)
    lanes[...] = column_to_lanes(jnp.sum(x * x, axis=1, keepdims=True))


def product(scaled, wk_ref, wv_ref):
    weight = jnp.concatenate([wk_ref[...], wv_ref[...]], axis=1)
    return jnp.dot(scaled[...], weight, preferred_element_type=F32)


def forward_other_kernel(place, x_ref, gain_ref, wk_ref, wv_ref, out_ref, scaled, lanes):
    @pl.when(pl.program_id(0) == 0)
    def _():
        prepare(x_ref, gain_ref, scaled, lanes)

    out_ref[0, 0:GROUP, :] = product(scaled, wk_ref, wv_ref).astype(BF16)
    out_ref[0, GROUP:, :] = split_extra(lanes[...])


def forward_own_kernel(
    place, x_ref, gain_ref, wk_ref, wv_ref, in_ref, out0, out1, out2, out3, scaled, lanes
):
    step = pl.program_id(0)

    @pl.when(step == 0)
    def _():
        prepare(x_ref, gain_ref, scaled, lanes)

    total = (product(scaled, wk_ref, wv_ref) + in_ref[0, 0:GROUP, :].astype(F32)).astype(BF16)
    extra = split_extra(lanes[...] + join_extra(in_ref[0, GROUP:, :]))
    for d, out_ref in enumerate((out0, out1, out2, out3)):

        @pl.when(step == d)
        def _(out_ref=out_ref):
            out_ref[0:GROUP, :] = total
            out_ref[GROUP:, :] = extra


def forward(place, x, block, gain, wk, wv, arrived=None):
    own = arrived is not None

    def columns(d, s):
        core = s[1] if own else 1 - s[1]
        return (0, 2 * lax.rem(s[0] + d, RINGS) + core)

    in_specs = [
        pl.BlockSpec((GROUP, x.shape[1]), lambda d, s: (block, 0)),
        pl.BlockSpec((1, x.shape[1]), lambda d, s: (0, 0)),
        pl.BlockSpec((wk.shape[0], HEAD), columns),
        pl.BlockSpec((wk.shape[0], HEAD), columns),
    ]
    operands = [x, gain, wk, wv]
    rows = GROUP + EXTRA
    if own:
        in_specs.append(pl.BlockSpec((1, rows, PAIR), lambda d, s: (d, 0, 0)))
        operands.append(arrived)
        out_shape = [jax.ShapeDtypeStruct((rows, PAIR), BF16)] * RINGS
        out_specs = [pl.BlockSpec((rows, PAIR), lambda d, s: (0, 0))] * RINGS
    else:
        out_shape = jax.ShapeDtypeStruct((RINGS, rows, PAIR), BF16)
        out_specs = pl.BlockSpec((1, rows, PAIR), lambda d, s: (d, 0, 0))
    return pl.pallas_call(
        forward_own_kernel if own else forward_other_kernel,
        grid_spec=pltpu.PrefetchScalarGridSpec(
            num_scalar_prefetch=1,
            grid=(RINGS,),
            in_specs=in_specs,
            out_specs=out_specs,
            scratch_shapes=[pltpu.VMEM((GROUP, x.shape[1]), BF16), pltpu.VMEM((8, HEAD), F32)],
        ),
        out_shape=out_shape,
        compiler_params=PARAMS,
        cost_estimate=pl.CostEstimate(
            flops=2 * GROUP * x.shape[1] * RINGS * PAIR, bytes_accessed=5 * 2**20, transcendentals=0
        ),
        name="forward_own" if own else "forward_other",
    )(place, *operands)


def gathered(refs):
    total = refs[0][0:GROUP, :].astype(F32)
    lanes = join_extra(refs[0][GROUP:, :])
    for ref in refs[1:]:
        total = total + ref[0:GROUP, :].astype(F32)
        lanes = lanes + join_extra(ref[GROUP:, :])
    inverse = lax.rsqrt(lanes_to_column(lanes) / WIDTH + EPSILON)
    return (inverse * total).astype(BF16), inverse


def residual(both, target, inverse, resid_ref, inverse_ref):
    resid = (both.astype(F32) - target).astype(BF16)
    dots = jnp.sum(resid.astype(F32) * both.astype(F32), axis=1, keepdims=True)
    resid_ref[0:GROUP, :] = resid
    resid_ref[GROUP:, :] = split_extra(column_to_lanes(dots))
    inverse_ref[...] = jnp.broadcast_to(inverse, (GROUP, HEAD))


def text_combine_kernel(a, b, c, d, kt_ref, vt_ref, keys_ref, values_ref, resid_ref, inverse_ref):
    both, inverse = gathered((a, b, c, d))
    target = jnp.concatenate([kt_ref[...], vt_ref[...]], axis=1).astype(F32)
    keys_ref[...] = both[:, 0:HEAD]
    values_ref[...] = both[:, HEAD:]
    residual(both, target, inverse, resid_ref, inverse_ref)


def one_hot(shape, match):
    return jnp.where(match, jnp.ones(shape, F32), jnp.zeros(shape, F32)).astype(BF16)


def slot_columns(rows, first, count, lanes_ref):
    row = first + lax.broadcasted_iota(jnp.int32, (rows, count), 0)
    begin = IMAGE_LEN * lax.broadcasted_iota(jnp.int32, (rows, count), 1)
    inside = (row >= begin) & (row < begin + IMAGE_LEN)
    value = lanes_ref[...] + (row - begin).astype(F32)
    return jnp.sum(jnp.where(inside, value, 0.0), axis=1, keepdims=True)


def slot_lanes(rows, count, column_ref):
    row = lax.broadcasted_iota(jnp.int32, (count, rows), 1)
    begin = IMAGE_LEN * lax.broadcasted_iota(jnp.int32, (count, rows), 0)
    inside = (row >= begin) & (row < begin + IMAGE_LEN)
    value = column_ref[...] + (row - begin).astype(F32)
    return jnp.sum(jnp.where(inside, value, 0.0), axis=0, keepdims=True)


def image_combine_kernel(
    a, b, c, d, arrived_ref, dest_lanes, dest_column, send_ref, resid_ref, inverse_ref
):
    slots = arrived_ref.shape[0]
    images = GROUP // IMAGE_LEN
    both, inverse = gathered((a, b, c, d))
    slot = slot_columns(GROUP, 0, images, dest_lanes)
    shape = (GROUP, slots)
    match = lax.broadcasted_iota(jnp.int32, shape, 1).astype(F32) == slot
    target = jnp.dot(one_hot(shape, match), arrived_ref[...], preferred_element_type=F32)
    residual(both, target, inverse, resid_ref, inverse_ref)
    shape = (slots, GROUP)
    match = lax.broadcasted_iota(jnp.int32, shape, 0).astype(F32) == slot_lanes(
        GROUP, images, dest_column
    )
    send_ref[...] = jnp.dot(one_hot(shape, match), both, preferred_element_type=F32).astype(BF16)


def combine(parts, targets, block):
    rows = GROUP + EXTRA
    part = pl.BlockSpec((rows, PAIR), lambda i: (0, 0))
    target = pl.BlockSpec((GROUP, HEAD), lambda i: (block, 0))
    head = pl.BlockSpec((GROUP, HEAD), lambda i: (0, 0))
    return pl.pallas_call(
        text_combine_kernel,
        grid=(1,),
        in_specs=[part] * RINGS + [target] * 2,
        out_specs=[head, head, part, head],
        out_shape=[
            jax.ShapeDtypeStruct((GROUP, HEAD), BF16),
            jax.ShapeDtypeStruct((GROUP, HEAD), BF16),
            jax.ShapeDtypeStruct((rows, PAIR), BF16),
            jax.ShapeDtypeStruct((GROUP, HEAD), F32),
        ],
        compiler_params=PARAMS,
        cost_estimate=pl.CostEstimate(flops=2**22, bytes_accessed=2**21, transcendentals=0),
        name="text_combine",
    )(*parts, *targets)


def image_combine(parts, arrived, dest):
    rows = GROUP + EXTRA
    return pl.pallas_call(
        image_combine_kernel,
        out_shape=[
            jax.ShapeDtypeStruct(arrived.shape, BF16),
            jax.ShapeDtypeStruct((rows, PAIR), BF16),
            jax.ShapeDtypeStruct((GROUP, HEAD), F32),
        ],
        compiler_params=PARAMS,
        cost_estimate=pl.CostEstimate(flops=2**28, bytes_accessed=2**21, transcendentals=0),
        name="image_combine",
    )(*parts, arrived, dest[None, :], dest[:, None])


def gather_kernel(first_ref, kt_ref, vt_ref, out_ref):
    rows, slots = kt_ref.shape[0], first_ref.shape[1]
    step = HEAD
    both = jnp.concatenate([kt_ref[...], vt_ref[...]], axis=1)
    for begin in range(0, out_ref.shape[0], step):
        place = slot_columns(step, begin, slots, first_ref)
        shape = (step, rows)
        match = lax.broadcasted_iota(jnp.int32, shape, 1).astype(F32) == place
        picked = jnp.dot(one_hot(shape, match), both, preferred_element_type=F32)
        out_ref[begin : begin + step, :] = picked.astype(BF16)


def gather_targets(first, key_target, value_target):
    slots = first.shape[0] * IMAGE_LEN
    return pl.pallas_call(
        gather_kernel,
        out_shape=jax.ShapeDtypeStruct((slots, PAIR), BF16),
        compiler_params=PARAMS,
        cost_estimate=pl.CostEstimate(flops=2**28, bytes_accessed=2**20, transcendentals=0),
        name="gather_targets",
    )(first[None, :], key_target, value_target)


def image_rows_mask(first_row, first_lanes):
    shape = (GROUP, first_lanes.shape[1])
    row = (first_row + lax.broadcasted_iota(jnp.int32, shape, 0)).astype(F32)
    begin = first_lanes[...]
    inside = (row >= begin) & (row < begin + IMAGE_LEN)
    return jnp.sum(jnp.where(inside, 1.0, 0.0), axis=1, keepdims=True) > 0.5


def merge_kernel(
    first_lanes, first_column, arrived_ref, k0, k1, v0, v1, keys_ref, values_ref
):
    slots = arrived_ref.shape[0]
    place = slot_lanes(slots, first_column.shape[0], first_column)
    for g, (k_ref, v_ref) in enumerate(((k0, v0), (k1, v1))):
        shape = (GROUP, slots)
        row = g * GROUP + lax.broadcasted_iota(jnp.int32, shape, 0)
        match = row.astype(F32) == place
        landed = jnp.dot(one_hot(shape, match), arrived_ref[...], preferred_element_type=F32)
        mask = image_rows_mask(g * GROUP, first_lanes)
        here = slice(g * GROUP, (g + 1) * GROUP)
        keys_ref[here, :] = jnp.where(mask, landed[:, 0:HEAD], k_ref[...].astype(F32)).astype(BF16)
        values_ref[here, :] = jnp.where(mask, landed[:, HEAD:], v_ref[...].astype(F32)).astype(BF16)


def merge(first, arrived, keys, values):
    rows = 2 * GROUP
    return pl.pallas_call(
        merge_kernel,
        out_shape=[jax.ShapeDtypeStruct((rows, HEAD), BF16)] * 2,
        compiler_params=PARAMS,
        cost_estimate=pl.CostEstimate(flops=2**28, bytes_accessed=2**21, transcendentals=0),
        name="merge",
    )(first[None, :], first[:, None], arrived, *keys, *values)


def backward_kernel(
    masked,
    aliased,
    block,
    place,
    x_ref,
    gain_ref,
    inverse_ref,
    first_lanes,
    wk_own,
    wv_own,
    wk_other,
    wv_other,
    *rest,
):
    resids = rest[0 : 2 * RINGS]
    out_ref, stacked, total, coefficient = rest[-4:]
    step = pl.program_id(0)

    @pl.when(step == 0)
    def _():
        lanes = jnp.zeros((8, HEAD), F32)
        for n, ref in enumerate(resids):
            core, d = n // RINGS, n % RINGS
            stacked[d, :, core * PAIR : (core + 1) * PAIR] = ref[0:GROUP, :]
            lanes = lanes + join_extra(ref[GROUP:, :])
        inverse = inverse_ref[...]
        column = lanes_to_column(lanes)
        coefficient[...] = inverse * inverse * column / WIDTH

    weight = jnp.concatenate([wk_own[...], wv_own[...], wk_other[...], wv_other[...]], axis=1)
    contract = (((1,), (1,)), ((), ()))
    back = lax.dot_general(stacked[step], weight, contract, preferred_element_type=F32)

    @pl.when(step == 0)
    def _():
        total[...] = back

    @pl.when((step > 0) & (step < RINGS - 1))
    def _():
        total[...] += back

    @pl.when(step == RINGS - 1)
    def _():
        inverse = inverse_ref[:, 0:1]
        grad = gain_ref[...] * inverse * (total[...] + back) - coefficient[:, 0:1] * x_ref[
            ...
        ].astype(F32)
        if masked:
            grad = jnp.where(image_rows_mask(block * GROUP, first_lanes), 0.0, grad)
        out_ref[...] = grad.astype(BF16)


def backward(place, x, block, gain, inverse, first, wk, wv, resids, masked, before=None):
    rows, width = GROUP + EXTRA, x.shape[1]

    def columns(other):
        def index(d, s):
            core = 1 - s[1] if other else s[1]
            return (0, 2 * lax.rem(s[0] + RINGS - d, RINGS) + core)

        return index

    weights = [pl.BlockSpec((width, HEAD), columns(other)) for other in (False, False, True, True)]
    in_specs = [
        pl.BlockSpec((GROUP, width), lambda d, s: (block, 0)),
        pl.BlockSpec((1, width), lambda d, s: (0, 0)),
        pl.BlockSpec((GROUP, HEAD), lambda d, s: (0, 0)),
        pl.BlockSpec((1, first.shape[0]), lambda d, s: (0, 0)),
        *weights,
        *[pl.BlockSpec((rows, PAIR), lambda d, s: (0, 0))] * (2 * RINGS),
    ]
    operands = [place, x, gain, inverse, first[None, :], wk, wv, wk, wv, *resids]
    aliases = {}
    if before is not None:
        in_specs.append(pl.BlockSpec(memory_space=pl.ANY))
        aliases = {len(operands): 0}
        operands.append(before)
    return pl.pallas_call(
        functools.partial(backward_kernel, masked, before is not None, block),
        grid_spec=pltpu.PrefetchScalarGridSpec(
            num_scalar_prefetch=1,
            grid=(RINGS,),
            in_specs=in_specs,
            out_specs=pl.BlockSpec((GROUP, width), lambda d, s: (block, 0)),
            scratch_shapes=[
                pltpu.VMEM((RINGS, GROUP, 2 * PAIR), BF16),
                pltpu.VMEM((GROUP, width), F32),
                pltpu.VMEM((GROUP, HEAD), F32),
            ],
        ),
        out_shape=jax.ShapeDtypeStruct(x.shape, BF16),
        input_output_aliases=aliases,
        compiler_params=PARAMS,
        cost_estimate=pl.CostEstimate(
            flops=2 * GROUP * width * 2 * RINGS * PAIR, bytes_accessed=8 * 2**20, transcendentals=0
        ),
        name="backward",
    )(*operands)


def around(x, shift):
    return lax.ppermute(
        x, "tp", [(2 * y + c, 2 * ((y + shift) % RINGS) + c) for y in range(RINGS) for c in range(2)]
    )


def across(x):
    return lax.ppermute(x, "tp", [(i, i ^ 1) for i in range(2 * RINGS)])


def on_device(
    text_embed,
    image_embed,
    image_start,
    norm_gain,
    key_weight,
    value_weight,
    key_target,
    value_target,
):
    shards = lax.axis_size("rows")
    myself = lax.axis_index("rows")
    mine = lax.axis_index("tp").astype(jnp.int32)
    place = jnp.stack([mine // 2, mine % 2])
    gain = norm_gain[None, :]
    starts = image_start.reshape(shards, -1)
    block_of = starts // text_embed.shape[0]
    offset = (starts - block_of * text_embed.shape[0]).astype(F32)
    here = jnp.where(block_of == myself, offset + 8192.0, 0.0)
    first = jnp.sum(here, axis=1) - 8192.0
    dest = IMAGE_LEN * lax.dynamic_index_in_dim(block_of, myself, 0, keepdims=False).astype(F32)

    inputs = [(text_embed, 0), (text_embed, 1), (image_embed, 0)]
    parts = []
    for x, block in inputs:
        other = forward(place, x, block, gain, key_weight, value_weight)
        own = forward(place, x, block, gain, key_weight, value_weight, across(other))
        parts.append([own[0]] + [around(own[d], d) for d in range(1, RINGS)])

    goals = gather_targets(first, key_target, value_target)
    goals = lax.all_to_all(goals, "rows", split_axis=0, concat_axis=0, tiled=True)
    k0, v0, *state0 = combine(parts[0], (key_target, value_target), 0)
    k1, v1, *state1 = combine(parts[1], (key_target, value_target), 1)
    send, *state2 = image_combine(parts[2], goals, dest)
    landed = lax.all_to_all(send, "rows", split_axis=0, concat_axis=0, tiled=True)

    grads = []
    for (x, block), (resid, inverse) in zip(inputs, (state0, state1, state2)):
        own = [resid] + [around(resid, d) for d in range(1, RINGS)]
        resids = own + [across(r) for r in own]
        before = grads[0] if len(grads) == 1 else None
        grads.append(
            backward(
                place, x, block, gain, inverse, first, key_weight, value_weight, resids,
                len(grads) < 2, before,
            )
        )
    keys, values = merge(first, landed, (k0, k1), (v0, v1))
    return (keys, values, grads[1], grads[2])


def solution(mesh):
    in_specs = (
        P("rows", "tp"),
        P("rows", "tp"),
        P(),
        P("tp"),
        P("tp", None),
        P("tp", None),
        P("rows", "tp"),
        P("rows", "tp"),
    )
    out_specs = (P("rows", "tp"), P("rows", "tp"), P("rows", "tp"), P("rows", "tp"))
    return jax.shard_map(
        on_device, mesh=mesh, in_specs=in_specs, out_specs=out_specs, check_vma=False
    )
```

```python
import functools

import jax
import jax.numpy as jnp
from jax import lax
from jax.experimental import pallas as pl
from jax.experimental.pallas import tpu as pltpu
from jax.sharding import PartitionSpec as P

WIDTH = 8192
EPSILON = 1e-06
IMAGE_LEN = 24
EXTRA = 16
HEAD = 128
PAIR = 2 * HEAD
RINGS = 4

F32 = jnp.float32
BF16 = jnp.bfloat16
PARAMS = pltpu.CompilerParams(vmem_limit_bytes=60 * 2**20)


def identity_mask():
    shape = (HEAD, HEAD)
    return lax.broadcasted_iota(jnp.int32, shape, 0) == lax.broadcasted_iota(jnp.int32, shape, 1)


def column_to_lanes(column):
    eye = identity_mask()
    row = lax.broadcasted_iota(jnp.int32, (8, HEAD), 0)
    out = jnp.zeros((8, HEAD), F32)
    for p in range(column.shape[0] // HEAD):
        piece = column[p * HEAD : (p + 1) * HEAD, :]
        lanes = jnp.sum(jnp.where(eye, piece, 0.0), axis=0, keepdims=True)
        out = jnp.where(row == p, lanes, out)
    return out


def lanes_to_column(lanes, rows):
    eye = identity_mask()
    pieces = [
        jnp.sum(jnp.where(eye, lanes[p : p + 1, :], 0.0), axis=1, keepdims=True)
        for p in range(rows // HEAD)
    ]
    return jnp.concatenate(pieces, axis=0)


def split_extra(lanes):
    high = lanes.astype(BF16).astype(F32)
    both = jnp.concatenate([high, lanes - high], axis=0)
    return jnp.concatenate([both, jnp.zeros((EXTRA, HEAD), F32)], axis=1).astype(BF16)


def join_extra(block):
    block = block.astype(F32)
    return block[0:8, 0:HEAD] + block[8:16, 0:HEAD]


def product(scaled_ref, wk_ref, wv_ref):
    weight = jnp.concatenate([wk_ref[...], wv_ref[...]], axis=1)
    return jnp.dot(scaled_ref[...], weight, preferred_element_type=F32)


def forward_other_kernel(place, x_ref, gain_ref, wk_ref, wv_ref, out_ref, scaled_ref, lanes_ref):
    @pl.when(pl.program_id(0) == 0)
    def _():
        x = x_ref[...].astype(F32)
        scaled_ref[...] = (gain_ref[...] * x).astype(BF16)
        lanes_ref[...] = column_to_lanes(jnp.sum(x * x, axis=1, keepdims=True))

    rows = x_ref.shape[0]
    out_ref[0, 0:rows, :] = product(scaled_ref, wk_ref, wv_ref).astype(BF16)
    out_ref[0, rows:, :] = split_extra(lanes_ref[...])


def forward_own_kernel(
    place, scaled_ref, lanes_ref, wk_ref, wv_ref, in_ref, out0, out1, out2, out3
):
    step, rows = pl.program_id(0), scaled_ref.shape[0]
    total = product(scaled_ref, wk_ref, wv_ref) + in_ref[0, 0:rows, :].astype(F32)
    total = total.astype(BF16)
    extra = split_extra(lanes_ref[...] + join_extra(in_ref[0, rows:, :]))
    for d, out_ref in enumerate((out0, out1, out2, out3)):

        @pl.when(step == d)
        def _(out_ref=out_ref):
            out_ref[0:rows, :] = total
            out_ref[rows:, :] = extra


def forward_call(kernel, own, place, operands, in_specs, out_specs, out_shape, rows, wk, wv):
    depth = wk.shape[0]

    def columns(d, s):
        core = s[1] if own else 1 - s[1]
        return (0, 2 * lax.rem(s[0] + d, RINGS) + core)

    weights = [pl.BlockSpec((depth, HEAD), columns)] * 2
    return pl.pallas_call(
        kernel,
        grid_spec=pltpu.PrefetchScalarGridSpec(
            num_scalar_prefetch=1,
            grid=(RINGS,),
            in_specs=in_specs[0:2] + weights + in_specs[2:],
            out_specs=out_specs,
        ),
        out_shape=out_shape,
        compiler_params=PARAMS,
        cost_estimate=pl.CostEstimate(
            flops=2 * rows * depth * RINGS * PAIR, bytes_accessed=rows * 2**13 + 2**21, transcendentals=0
        ),
        name="forward_own" if own else "forward_other",
    )(place, *operands[0:2], wk, wv, *operands[2:])


def whole(shape):
    return pl.BlockSpec(shape, lambda *_: (0,) * len(shape))


def stepwise(shape):
    return pl.BlockSpec((1,) + shape, lambda d, s: (d, 0, 0))


def forward_other(place, x, gain, wk, wv):
    rows, width = x.shape
    block = (rows + EXTRA, PAIR)
    return forward_call(
        forward_other_kernel,
        False,
        place,
        (x, gain),
        [whole(x.shape), whole(gain.shape)],
        [stepwise(block), whole(x.shape), whole((8, HEAD))],
        [
            jax.ShapeDtypeStruct((RINGS,) + block, BF16),
            jax.ShapeDtypeStruct(x.shape, BF16),
            jax.ShapeDtypeStruct((8, HEAD), F32),
        ],
        rows,
        wk,
        wv,
    )


def forward_own(place, scaled, lanes, wk, wv, arrived):
    rows = scaled.shape[0]
    block = (rows + EXTRA, PAIR)
    return forward_call(
        forward_own_kernel,
        True,
        place,
        (scaled, lanes, arrived),
        [whole(scaled.shape), whole(lanes.shape), stepwise(block)],
        [whole(block)] * RINGS,
        [jax.ShapeDtypeStruct(block, BF16)] * RINGS,
        rows,
        wk,
        wv,
    )


def gathered(refs):
    rows = refs[0].shape[0] - EXTRA
    total = refs[0][0:rows, :].astype(F32)
    lanes = join_extra(refs[0][rows:, :])
    for ref in refs[1:]:
        total = total + ref[0:rows, :].astype(F32)
        lanes = lanes + join_extra(ref[rows:, :])
    inverse = lax.rsqrt(lanes_to_column(lanes, rows) / WIDTH + EPSILON)
    return (inverse * total).astype(BF16), inverse


def residual(both, target, inverse, resid_ref, inverse_ref):
    rows = both.shape[0]
    resid = (both.astype(F32) - target).astype(BF16)
    dots = jnp.sum(resid.astype(F32) * both.astype(F32), axis=1, keepdims=True)
    resid_ref[0:rows, :] = resid
    resid_ref[rows:, :] = split_extra(column_to_lanes(dots))
    inverse_ref[...] = jnp.broadcast_to(inverse, (rows, HEAD))


def text_combine_kernel(a, b, c, d, kt_ref, vt_ref, keys_ref, values_ref, resid_ref, inverse_ref):
    both, inverse = gathered((a, b, c, d))
    target = jnp.concatenate([kt_ref[...], vt_ref[...]], axis=1).astype(F32)
    keys_ref[...] = both[:, 0:HEAD]
    values_ref[...] = both[:, HEAD:]
    residual(both, target, inverse, resid_ref, inverse_ref)


def one_hot(shape, match):
    return jnp.where(match, jnp.ones(shape, F32), jnp.zeros(shape, F32)).astype(BF16)


def slot_columns(rows, first, count, lanes_ref):
    row = first + lax.broadcasted_iota(jnp.int32, (rows, count), 0)
    begin = IMAGE_LEN * lax.broadcasted_iota(jnp.int32, (rows, count), 1)
    inside = (row >= begin) & (row < begin + IMAGE_LEN)
    value = lanes_ref[...] + (row - begin).astype(F32)
    return jnp.sum(jnp.where(inside, value, 0.0), axis=1, keepdims=True)


def slot_lanes(rows, count, column_ref):
    row = lax.broadcasted_iota(jnp.int32, (count, rows), 1)
    begin = IMAGE_LEN * lax.broadcasted_iota(jnp.int32, (count, rows), 0)
    inside = (row >= begin) & (row < begin + IMAGE_LEN)
    value = column_ref[...] + (row - begin).astype(F32)
    return jnp.sum(jnp.where(inside, value, 0.0), axis=0, keepdims=True)


def image_combine_kernel(
    a, b, c, d, arrived_ref, dest_lanes, dest_column, send_ref, resid_ref, inverse_ref
):
    slots, images = arrived_ref.shape[0], dest_lanes.shape[1]
    rows = images * IMAGE_LEN
    both, inverse = gathered((a, b, c, d))
    slot = slot_columns(rows, 0, images, dest_lanes)
    shape = (rows, slots)
    match = lax.broadcasted_iota(jnp.int32, shape, 1).astype(F32) == slot
    target = jnp.dot(one_hot(shape, match), arrived_ref[...], preferred_element_type=F32)
    residual(both, target, inverse, resid_ref, inverse_ref)
    shape = (slots, rows)
    match = lax.broadcasted_iota(jnp.int32, shape, 0).astype(F32) == slot_lanes(
        rows, images, dest_column
    )
    send_ref[...] = jnp.dot(one_hot(shape, match), both, preferred_element_type=F32).astype(BF16)


def text_combine(parts, targets):
    rows = targets[0].shape[0]
    return pl.pallas_call(
        text_combine_kernel,
        out_shape=[
            jax.ShapeDtypeStruct((rows, HEAD), BF16),
            jax.ShapeDtypeStruct((rows, HEAD), BF16),
            jax.ShapeDtypeStruct(parts[0].shape, BF16),
            jax.ShapeDtypeStruct((rows, HEAD), F32),
        ],
        compiler_params=PARAMS,
        cost_estimate=pl.CostEstimate(flops=2**22, bytes_accessed=2**22, transcendentals=0),
        name="text_combine",
    )(*parts, *targets)


def image_combine(parts, arrived, dest):
    rows = parts[0].shape[0] - EXTRA
    return pl.pallas_call(
        image_combine_kernel,
        out_shape=[
            jax.ShapeDtypeStruct(arrived.shape, BF16),
            jax.ShapeDtypeStruct(parts[0].shape, BF16),
            jax.ShapeDtypeStruct((rows, HEAD), F32),
        ],
        compiler_params=PARAMS,
        cost_estimate=pl.CostEstimate(flops=2**28, bytes_accessed=2**21, transcendentals=0),
        name="image_combine",
    )(*parts, arrived, dest[None, :], dest[:, None])


def gather_kernel(first_ref, kt_ref, vt_ref, out_ref):
    rows, slots = kt_ref.shape[0], first_ref.shape[1]
    step = HEAD
    both = jnp.concatenate([kt_ref[...], vt_ref[...]], axis=1)
    for begin in range(0, out_ref.shape[0], step):
        place = slot_columns(step, begin, slots, first_ref)
        shape = (step, rows)
        match = lax.broadcasted_iota(jnp.int32, shape, 1).astype(F32) == place
        picked = jnp.dot(one_hot(shape, match), both, preferred_element_type=F32)
        out_ref[begin : begin + step, :] = picked.astype(BF16)


def gather_targets(first, key_target, value_target):
    slots = first.shape[0] * IMAGE_LEN
    return pl.pallas_call(
        gather_kernel,
        out_shape=jax.ShapeDtypeStruct((slots, PAIR), BF16),
        compiler_params=PARAMS,
        cost_estimate=pl.CostEstimate(flops=2**28, bytes_accessed=2**20, transcendentals=0),
        name="gather_targets",
    )(first[None, :], key_target, value_target)


def image_rows_mask(rows, first_row, first_lanes):
    shape = (rows, first_lanes.shape[1])
    row = (first_row + lax.broadcasted_iota(jnp.int32, shape, 0)).astype(F32)
    begin = first_lanes[...]
    inside = (row >= begin) & (row < begin + IMAGE_LEN)
    return jnp.sum(jnp.where(inside, 1.0, 0.0), axis=1, keepdims=True) > 0.5


def merge_kernel(first_lanes, first_column, arrived_ref, k_ref, v_ref, keys_ref, values_ref):
    slots = arrived_ref.shape[0]
    place = slot_lanes(slots, first_column.shape[0], first_column)
    step = 2 * HEAD
    for begin in range(0, k_ref.shape[0], step):
        shape = (step, slots)
        row = begin + lax.broadcasted_iota(jnp.int32, shape, 0)
        match = row.astype(F32) == place
        landed = jnp.dot(one_hot(shape, match), arrived_ref[...], preferred_element_type=F32)
        mask = image_rows_mask(step, begin, first_lanes)
        here = slice(begin, begin + step)
        keys = jnp.where(mask, landed[:, 0:HEAD], k_ref[here, :].astype(F32))
        values = jnp.where(mask, landed[:, HEAD:], v_ref[here, :].astype(F32))
        keys_ref[here, :] = keys.astype(BF16)
        values_ref[here, :] = values.astype(BF16)


def merge(first, arrived, keys, values):
    return pl.pallas_call(
        merge_kernel,
        out_shape=[jax.ShapeDtypeStruct(keys.shape, BF16)] * 2,
        compiler_params=PARAMS,
        cost_estimate=pl.CostEstimate(flops=2**28, bytes_accessed=2**21, transcendentals=0),
        name="merge",
    )(first[None, :], first[:, None], arrived, keys, values)


def backward_kernel(masked, place, x_ref, gain_ref, inverse_ref, first_lanes, wk_ref, wv_ref, *rest):
    resids = rest[0 : 2 * RINGS]
    out_ref, keys_all, values_all, coefficient, keep = rest[2 * RINGS :]
    rows = x_ref.shape[0]

    @pl.when(pl.program_id(0) == 0)
    def _():
        lanes = jnp.zeros((8, HEAD), F32)
        for n, ref in enumerate(resids):
            other, d = n // RINGS, n % RINGS
            core = 1 - place[1] if other else place[1]
            begin = HEAD * (2 * lax.rem(place[0] + RINGS - d, RINGS) + core)
            columns = pl.ds(pl.multiple_of(begin, HEAD), HEAD)
            keys_all[:, columns] = ref[0:rows, 0:HEAD]
            values_all[:, columns] = ref[0:rows, HEAD:]
            lanes = lanes + join_extra(ref[rows:, :])
        inverse = inverse_ref[...]
        coefficient[...] = inverse * inverse * lanes_to_column(lanes, rows) / WIDTH
        if masked:
            mask = image_rows_mask(rows, 0, first_lanes)
            keep[...] = jnp.broadcast_to(jnp.where(mask, 0.0, 1.0), keep.shape)

    contract = (((1,), (1,)), ((), ()))
    back = lax.dot_general(keys_all[...], wk_ref[...], contract, preferred_element_type=F32)
    back += lax.dot_general(values_all[...], wv_ref[...], contract, preferred_element_type=F32)
    grad = gain_ref[...] * inverse_ref[:, 0:1] * back
    grad = grad - coefficient[:, 0:1] * x_ref[...].astype(F32)
    if masked:
        grad = jnp.where(keep[:, 0:1] > 0.5, grad, 0.0)
    out_ref[...] = grad.astype(BF16)


def backward(place, x, gain, inverse, first, wk, wv, resids, masked):
    rows, width = x.shape
    columns = wk.shape[1]
    tile = 256
    across_tiles = lambda shape: pl.BlockSpec(shape, lambda i, s: (0, i))
    return pl.pallas_call(
        functools.partial(backward_kernel, masked),
        grid_spec=pltpu.PrefetchScalarGridSpec(
            num_scalar_prefetch=1,
            grid=(width // tile,),
            in_specs=[
                across_tiles((rows, tile)),
                across_tiles((1, tile)),
                whole((rows, HEAD)),
                whole((1, first.shape[0])),
                pl.BlockSpec((tile, columns), lambda i, s: (i, 0)),
                pl.BlockSpec((tile, columns), lambda i, s: (i, 0)),
                *[whole(resids[0].shape)] * (2 * RINGS),
            ],
            out_specs=across_tiles((rows, tile)),
            scratch_shapes=[
                pltpu.VMEM((rows, columns), BF16),
                pltpu.VMEM((rows, columns), BF16),
                pltpu.VMEM((rows, HEAD), F32),
                pltpu.VMEM((rows, HEAD), F32),
            ],
        ),
        out_shape=jax.ShapeDtypeStruct(x.shape, BF16),
        compiler_params=PARAMS,
        cost_estimate=pl.CostEstimate(
            flops=4 * rows * width * columns, bytes_accessed=rows * 2**13 + 2**22, transcendentals=0
        ),
        name="backward",
    )(place, x, gain, inverse, first[None, :], wk, wv, *resids)


def around(x, shift):
    return lax.ppermute(
        x, "tp", [(2 * y + c, 2 * ((y + shift) % RINGS) + c) for y in range(RINGS) for c in range(2)]
    )


def across(x):
    return lax.ppermute(x, "tp", [(i, i ^ 1) for i in range(2 * RINGS)])


def on_device(
    text_embed,
    image_embed,
    image_start,
    norm_gain,
    key_weight,
    value_weight,
    key_target,
    value_target,
):
    shards = lax.axis_size("rows")
    myself = lax.axis_index("rows")
    mine = lax.axis_index("tp").astype(jnp.int32)
    place = jnp.stack([mine // 2, mine % 2])
    gain = norm_gain[None, :]
    starts = image_start.reshape(shards, -1)
    block_of = starts // text_embed.shape[0]
    offset = (starts - block_of * text_embed.shape[0]).astype(F32)
    here = jnp.where(block_of == myself, offset + 8192.0, 0.0)
    first = jnp.sum(here, axis=1) - 8192.0
    dest = IMAGE_LEN * lax.dynamic_index_in_dim(block_of, myself, 0, keepdims=False).astype(F32)

    inputs = (text_embed, image_embed)
    parts = []
    for x in inputs:
        other, scaled, lanes = forward_other(place, x, gain, key_weight, value_weight)
        own = forward_own(place, scaled, lanes, key_weight, value_weight, across(other))
        parts.append([own[0]] + [around(own[d], d) for d in range(1, RINGS)])

    goals = gather_targets(first, key_target, value_target)
    goals = lax.all_to_all(goals, "rows", split_axis=0, concat_axis=0, tiled=True)
    keys, values, *text_state = text_combine(parts[0], (key_target, value_target))
    send, *image_state = image_combine(parts[1], goals, dest)
    landed = lax.all_to_all(send, "rows", split_axis=0, concat_axis=0, tiled=True)

    grads = []
    for n, (x, (resid, inverse)) in enumerate(zip(inputs, (text_state, image_state))):
        own = [resid] + [around(resid, d) for d in range(1, RINGS)]
        resids = own + [across(r) for r in own]
        grads.append(
            backward(place, x, gain, inverse, first, key_weight, value_weight, resids, n == 0)
        )
    keys, values = merge(first, landed, keys, values)
    return (keys, values, *grads)


def solution(mesh):
    in_specs = (
        P("rows", "tp"),
        P("rows", "tp"),
        P(),
        P("tp"),
        P("tp", None),
        P("tp", None),
        P("rows", "tp"),
        P("rows", "tp"),
    )
    out_specs = (P("rows", "tp"), P("rows", "tp"), P("rows", "tp"), P("rows", "tp"))
    return jax.shard_map(
        on_device, mesh=mesh, in_specs=in_specs, out_specs=out_specs, check_vma=False
    )
```

```python
import functools

import jax
import jax.numpy as jnp
from jax import lax
from jax.experimental import pallas as pl
from jax.experimental.pallas import tpu as pltpu
from jax.sharding import PartitionSpec as P

WIDTH = 8192
EPSILON = 1e-06
IMAGE_LEN = 24
EXTRA = 16
HEAD = 128
PAIR = 2 * HEAD
RINGS = 4
CHUNKS = 2 * RINGS
PIECE = 128
ABSENT = 8192.0

F32 = jnp.float32
BF16 = jnp.bfloat16
PARAMS = pltpu.CompilerParams(vmem_limit_bytes=20 * 2**20)
IN_VMEM = pl.BlockSpec(memory_space=pltpu.VMEM)
ANYWHERE = pl.BlockSpec(memory_space=pl.ANY)


def near(x):
    return pltpu.with_memory_space_constraint(x, pltpu.VMEM)


def cost(flops, nbytes):
    return pl.CostEstimate(flops=flops, bytes_accessed=nbytes, transcendentals=0)


def same_index(count):
    shape = (count, count)
    return lax.broadcasted_iota(jnp.int32, shape, 0) == lax.broadcasted_iota(jnp.int32, shape, 1)


def column_to_lanes(column):
    eye = same_index(HEAD)
    row = lax.broadcasted_iota(jnp.int32, (8, HEAD), 0)
    out = jnp.zeros((8, HEAD), F32)
    for p in range(column.shape[0] // HEAD):
        piece = column[p * HEAD : (p + 1) * HEAD, :]
        lanes = jnp.sum(jnp.where(eye, piece, 0.0), axis=0, keepdims=True)
        out = jnp.where(row == p, lanes, out)
    return out


def lanes_to_column(lanes, rows):
    eye = same_index(HEAD)
    pieces = [
        jnp.sum(jnp.where(eye, lanes[p : p + 1, :], 0.0), axis=1, keepdims=True)
        for p in range(rows // HEAD)
    ]
    return jnp.concatenate(pieces, axis=0)


def split_extra(lanes):
    high = lanes.astype(BF16).astype(F32)
    both = jnp.concatenate([high, lanes - high], axis=0)
    return jnp.concatenate([both, jnp.zeros((EXTRA, HEAD), F32)], axis=1).astype(BF16)


def join_extra(block):
    block = block.astype(F32)
    return block[0:8, 0:HEAD] + block[8:16, 0:HEAD]


def my_place():
    mine = lax.axis_index("tp")
    return lax.div(mine, 2), lax.rem(mine, 2)


def weight_copies(wk_ref, wv_ref, weight_ref, sems):
    ring, core = my_place()
    copies = []
    for j in range(CHUNKS):
        chip = lax.rem(ring + j % RINGS, RINGS)
        begin = pl.multiple_of(HEAD * (2 * chip + (core if j < RINGS else 1 - core)), HEAD)
        copies.append(
            [
                pltpu.make_async_copy(
                    ref.at[:, pl.ds(begin, HEAD)],
                    weight_ref.at[:, pl.ds(j * PAIR + n * HEAD, HEAD)],
                    sems.at[2 * j + n],
                )
                for n, ref in enumerate((wk_ref, wv_ref))
            ]
        )
    return copies


def forward_other_kernel(loads, x_ref, gain_ref, *refs):
    if loads:
        wk_ref, wv_ref, send_ref, scaled_ref, lanes_ref, held_ref, weight_ref, sems, more = refs
    else:
        weight_ref, send_ref, scaled_ref, lanes_ref, held_ref, sems = refs
    rows = x_ref.shape[0]
    x_copies = []
    for p in range(rows // PIECE):
        here = pl.ds(p * PIECE, PIECE)
        x_copies.append(pltpu.make_async_copy(x_ref.at[here], held_ref.at[here], sems.at[p]))
        x_copies[-1].start()
    weights = weight_copies(wk_ref, wv_ref, weight_ref, more) if loads else []
    for pair in weights[RINGS:] + weights[:RINGS]:
        for copy in pair:
            copy.start()
    row = lax.broadcasted_iota(jnp.int32, (8, HEAD), 0)
    eye = same_index(HEAD)
    lanes = jnp.zeros((8, HEAD), F32)
    for p, copy in enumerate(x_copies):
        copy.wait()
        here = slice(p * PIECE, (p + 1) * PIECE)
        x = held_ref[here, :].astype(F32)
        scaled_ref[here, :] = (gain_ref[...] * x).astype(BF16)
        squares = jnp.sum(x * x, axis=1, keepdims=True)
        line = jnp.sum(jnp.where(eye, squares, 0.0), axis=0, keepdims=True)
        lanes = jnp.where(row == p, line, lanes)
    lanes_ref[...] = lanes
    extra = split_extra(lanes)
    for d in range(RINGS):
        if loads:
            for copy in weights[RINGS + d]:
                copy.wait()
        weight = weight_ref[:, (RINGS + d) * PAIR : (RINGS + d + 1) * PAIR]
        product = jnp.dot(scaled_ref[...], weight, preferred_element_type=F32)
        send_ref[d, 0:rows, :] = product.astype(BF16)
        send_ref[d, rows:, :] = extra
    if loads:
        for pair in weights[:RINGS]:
            for copy in pair:
                copy.wait()


def forward_other(x, gain, weights):
    rows, width = x.shape
    loads = len(weights) == 2
    out_shape = [
        pltpu.VMEM((RINGS, rows + EXTRA, PAIR), BF16),
        pltpu.VMEM(x.shape, BF16),
        pltpu.VMEM((8, HEAD), F32),
        pltpu.VMEM(x.shape, BF16),
    ]
    scratch = [pltpu.SemaphoreType.DMA((rows // PIECE,))]
    if loads:
        out_shape.append(pltpu.VMEM((width, CHUNKS * PAIR), BF16))
        scratch.append(pltpu.SemaphoreType.DMA((2 * CHUNKS,)))
    else:
        weights = [near(w) for w in weights]
    return pl.pallas_call(
        functools.partial(forward_other_kernel, loads),
        in_specs=[ANYWHERE, IN_VMEM] + [ANYWHERE if loads else IN_VMEM] * len(weights),
        out_specs=[IN_VMEM] * len(out_shape),
        out_shape=out_shape,
        scratch_shapes=scratch,
        compiler_params=PARAMS,
        cost_estimate=cost(2 * rows * width * RINGS * PAIR, 2**22 if loads else 2**20),
        name="forward_other",
    )(x, gain, *weights)


def forward_own_kernel(scaled_ref, lanes_ref, weight_ref, in_ref, *out_refs):
    rows = scaled_ref.shape[0]
    extra = split_extra(lanes_ref[...] + join_extra(in_ref[0, rows:, :]))
    for d, out_ref in enumerate(out_refs):
        weight = weight_ref[:, d * PAIR : (d + 1) * PAIR]
        product = jnp.dot(scaled_ref[...], weight, preferred_element_type=F32)
        out_ref[0:rows, :] = (product + in_ref[d, 0:rows, :].astype(F32)).astype(BF16)
        out_ref[rows:, :] = extra


def forward_own(scaled, lanes, weight, arrived):
    rows, width = scaled.shape
    return pl.pallas_call(
        forward_own_kernel,
        in_specs=[IN_VMEM] * 4,
        out_specs=[IN_VMEM] * RINGS,
        out_shape=[pltpu.VMEM((rows + EXTRA, PAIR), BF16)] * RINGS,
        compiler_params=PARAMS,
        cost_estimate=cost(2 * rows * width * RINGS * PAIR, 2**20),
        name="forward_own",
    )(near(scaled), near(lanes), near(weight), near(arrived))


def gathered(refs):
    rows = refs[0].shape[0] - EXTRA
    total = refs[0][0:rows, :].astype(F32)
    lanes = join_extra(refs[0][rows:, :])
    for ref in refs[1:]:
        total = total + ref[0:rows, :].astype(F32)
        lanes = lanes + join_extra(ref[rows:, :])
    inverse = lax.rsqrt(lanes_to_column(lanes, rows) / WIDTH + EPSILON)
    return (inverse * total).astype(BF16), inverse


def residual(both, target, resid_ref):
    rows = both.shape[0]
    both = both.astype(F32)
    resid = (both - target.astype(F32)).astype(BF16)
    dots = jnp.sum(resid.astype(F32) * both, axis=1, keepdims=True)
    resid_ref[0:rows, :] = resid
    resid_ref[rows:, :] = split_extra(column_to_lanes(dots))


def text_combine_kernel(a, b, c, d, target_ref, both_ref, resid_ref, inverse_ref):
    both, inverse = gathered((a, b, c, d))
    both_ref[...] = both
    inverse_ref[...] = jnp.broadcast_to(inverse, inverse_ref.shape)
    residual(both, target_ref[...], resid_ref)


def text_combine(parts, target):
    rows = target.shape[0]
    return pl.pallas_call(
        text_combine_kernel,
        in_specs=[IN_VMEM] * 5,
        out_specs=[IN_VMEM] * 3,
        out_shape=[
            pltpu.VMEM((rows, PAIR), BF16),
            pltpu.VMEM(parts[0].shape, BF16),
            pltpu.VMEM((rows, HEAD), F32),
        ],
        compiler_params=PARAMS,
        cost_estimate=cost(2**22, 2**22),
        name="text_combine",
    )(*[near(p) for p in parts], near(target))


def one_hot(match):
    return jnp.where(match, jnp.ones(match.shape, F32), jnp.zeros(match.shape, F32)).astype(BF16)


def slot_columns(rows, first, lanes):
    shape = (rows, lanes.shape[1])
    row = first + lax.broadcasted_iota(jnp.int32, shape, 0)
    begin = IMAGE_LEN * lax.broadcasted_iota(jnp.int32, shape, 1)
    inside = (row >= begin) & (row < begin + IMAGE_LEN)
    value = lanes + (row - begin).astype(F32)
    return jnp.sum(jnp.where(inside, value, 0.0), axis=1, keepdims=True)


def slot_lanes(rows, column):
    shape = (column.shape[0], rows)
    row = lax.broadcasted_iota(jnp.int32, shape, 1)
    begin = IMAGE_LEN * lax.broadcasted_iota(jnp.int32, shape, 0)
    inside = (row >= begin) & (row < begin + IMAGE_LEN)
    value = column + (row - begin).astype(F32)
    return jnp.sum(jnp.where(inside, value, 0.0), axis=0, keepdims=True)


def first_rows(starts_ref, rows):
    start = starts_ref[...].astype(F32)
    offset = start - (lax.axis_index("rows") * rows).astype(F32)
    inside = (offset >= 0.0) & (offset < rows)
    column = jnp.sum(jnp.where(inside, offset + ABSENT, 0.0), axis=1, keepdims=True) - ABSENT
    eye = same_index(column.shape[0])
    return column, jnp.sum(jnp.where(eye, column, 0.0), axis=0, keepdims=True)


def destinations(starts_ref, rows):
    start = starts_ref[...].astype(F32)
    block = jnp.floor((start + 0.5) / rows)
    source = lax.broadcasted_iota(jnp.int32, start.shape, 0)
    mine = source == lax.axis_index("rows")
    lanes = IMAGE_LEN * jnp.sum(jnp.where(mine, block, 0.0), axis=0, keepdims=True)
    eye = same_index(lanes.shape[1])
    return lanes, jnp.sum(jnp.where(eye, lanes, 0.0), axis=1, keepdims=True)


def image_keys_kernel(seq_rows, a, b, c, d, starts_ref, send_ref, both_ref, inverse_ref):
    both, inverse = gathered((a, b, c, d))
    both_ref[...] = both
    inverse_ref[...] = jnp.broadcast_to(inverse, inverse_ref.shape)
    _, dest = destinations(starts_ref, seq_rows)
    shape = (send_ref.shape[0], both.shape[0])
    slot = lax.broadcasted_iota(jnp.int32, shape, 0).astype(F32)
    picks = one_hot(slot == slot_lanes(both.shape[0], dest))
    send_ref[...] = jnp.dot(picks, both, preferred_element_type=F32).astype(BF16)


def image_keys(parts, starts, seq_rows):
    rows = parts[0].shape[0] - EXTRA
    return pl.pallas_call(
        functools.partial(image_keys_kernel, seq_rows),
        in_specs=[IN_VMEM] * 5,
        out_specs=[IN_VMEM] * 3,
        out_shape=[
            jax.ShapeDtypeStruct((starts.shape[0] * IMAGE_LEN, PAIR), BF16),
            pltpu.VMEM((rows, PAIR), BF16),
            pltpu.VMEM((rows, HEAD), F32),
        ],
        compiler_params=PARAMS,
        cost_estimate=cost(2**28, 2**20),
        name="image_keys",
    )(*[near(p) for p in parts], starts)


def image_residual_kernel(seq_rows, both_ref, arrived_ref, starts_ref, resid_ref):
    rows = both_ref.shape[0]
    dest, _ = destinations(starts_ref, seq_rows)
    shape = (rows, arrived_ref.shape[0])
    slot = lax.broadcasted_iota(jnp.int32, shape, 1).astype(F32)
    picks = one_hot(slot == slot_columns(rows, 0, dest))
    target = jnp.dot(picks, arrived_ref[...], preferred_element_type=F32)
    residual(both_ref[...], target, resid_ref)


def image_residual(both, arrived, starts, seq_rows):
    return pl.pallas_call(
        functools.partial(image_residual_kernel, seq_rows),
        in_specs=[IN_VMEM] * 3,
        out_specs=IN_VMEM,
        out_shape=pltpu.VMEM((both.shape[0] + EXTRA, PAIR), BF16),
        compiler_params=PARAMS,
        cost_estimate=cost(2**28, 2**20),
        name="image_residual",
    )(near(both), near(arrived), starts)


def gather_kernel(starts_ref, kt_ref, vt_ref, out_ref, target_ref):
    rows = kt_ref.shape[0]
    target_ref[:, 0:HEAD] = kt_ref[...]
    target_ref[:, HEAD:] = vt_ref[...]
    _, first = first_rows(starts_ref, rows)
    for begin in range(0, out_ref.shape[0], PAIR):
        place = slot_columns(PAIR, begin, first)
        position = lax.broadcasted_iota(jnp.int32, (PAIR, rows), 1).astype(F32)
        picked = jnp.dot(
            one_hot(position == place), target_ref[...], preferred_element_type=F32
        )
        out_ref[begin : begin + PAIR, :] = picked.astype(BF16)


def gather_targets(starts, key_target, value_target):
    rows = key_target.shape[0]
    return pl.pallas_call(
        gather_kernel,
        in_specs=[IN_VMEM] * 3,
        out_specs=[IN_VMEM] * 2,
        out_shape=[
            jax.ShapeDtypeStruct((starts.shape[0] * IMAGE_LEN, PAIR), BF16),
            pltpu.VMEM((rows, PAIR), BF16),
        ],
        compiler_params=PARAMS,
        cost_estimate=cost(2**28, 2**20),
        name="gather_targets",
    )(starts, key_target, value_target)


def image_rows_mask(rows, first_row, first_lanes):
    shape = (rows, first_lanes.shape[1])
    row = (first_row + lax.broadcasted_iota(jnp.int32, shape, 0)).astype(F32)
    inside = (row >= first_lanes) & (row < first_lanes + IMAGE_LEN)
    return jnp.sum(jnp.where(inside, 1.0, 0.0), axis=1, keepdims=True) > 0.5


def merge_kernel(starts_ref, arrived_ref, both_ref, keys_ref, values_ref):
    slots, rows = arrived_ref.shape[0], both_ref.shape[0]
    column, lanes = first_rows(starts_ref, rows)
    place = slot_lanes(slots, column)
    for begin in range(0, rows, PAIR):
        row = begin + lax.broadcasted_iota(jnp.int32, (PAIR, slots), 0)
        picks = one_hot(row.astype(F32) == place)
        landed = jnp.dot(picks, arrived_ref[...], preferred_element_type=F32)
        here = slice(begin, begin + PAIR)
        mask = image_rows_mask(PAIR, begin, lanes)
        both = jnp.where(mask, landed, both_ref[here, :].astype(F32)).astype(BF16)
        keys_ref[here, :] = both[:, 0:HEAD]
        values_ref[here, :] = both[:, HEAD:]


def merge(starts, arrived, both):
    rows = both.shape[0]
    return pl.pallas_call(
        merge_kernel,
        in_specs=[IN_VMEM] * 3,
        out_specs=[IN_VMEM] * 2,
        out_shape=[jax.ShapeDtypeStruct((rows, HEAD), BF16)] * 2,
        compiler_params=PARAMS,
        cost_estimate=cost(2**28, 2**20),
        name="merge",
    )(starts, near(arrived), near(both))


def backward_kernel(masked, tile, x_ref, gain_ref, inverse_ref, weight_ref, *rest):
    rest = list(rest)
    starts_ref = rest.pop(0) if masked else None
    resids = rest[0:CHUNKS]
    out_ref, stacked, held, sems = rest[CHUNKS:]
    rows, width = x_ref.shape
    lanes = jnp.zeros((8, HEAD), F32)
    for n, ref in enumerate(resids):
        chunk = (RINGS - n) % RINGS + RINGS * (n // RINGS)
        stacked[:, chunk * PAIR : (chunk + 1) * PAIR] = ref[0:rows, :]
        lanes = lanes + join_extra(ref[rows:, :])
    inverse = inverse_ref[:, 0:1]
    coefficient = inverse * inverse * lanes_to_column(lanes, rows) / WIDTH
    if masked:
        mask = image_rows_mask(rows, 0, first_rows(starts_ref, rows)[1])
    contract = (((1,), (1,)), ((), ()))
    copies = []
    for n in range(width // tile):
        here = slice(n * tile, (n + 1) * tile)
        back = lax.dot_general(
            stacked[...], weight_ref[here, :], contract, preferred_element_type=F32
        )
        grad = gain_ref[:, here] * inverse * back - coefficient * x_ref[:, here].astype(F32)
        if masked:
            grad = jnp.where(mask, 0.0, grad)
        held[:, here] = grad.astype(BF16)
        span = pl.ds(n * tile, tile)
        copies.append(pltpu.make_async_copy(held.at[:, span], out_ref.at[:, span], sems.at[n]))
        copies[-1].start()
    for copy in copies:
        copy.wait()


def backward(x, gain, inverse, weight, starts, resids):
    rows, width = x.shape
    tile = 256
    masked = starts is not None
    operands = [near(x), gain, near(inverse), near(weight)] + ([starts] if masked else [])
    operands += [near(r) for r in resids]
    return pl.pallas_call(
        functools.partial(backward_kernel, masked, tile),
        in_specs=[IN_VMEM] * len(operands),
        out_specs=ANYWHERE,
        out_shape=jax.ShapeDtypeStruct(x.shape, BF16),
        scratch_shapes=[
            pltpu.VMEM((rows, CHUNKS * PAIR), BF16),
            pltpu.VMEM((rows, width), BF16),
            pltpu.SemaphoreType.DMA((width // tile,)),
        ],
        compiler_params=PARAMS,
        cost_estimate=cost(2 * rows * width * CHUNKS * PAIR, 2**21),
        name="backward",
    )(*operands)


def around(x, shift):
    return lax.ppermute(
        x, "tp", [(2 * y + c, 2 * ((y + shift) % RINGS) + c) for y in range(RINGS) for c in range(2)]
    )


def across(x):
    return lax.ppermute(x, "tp", [(i, i ^ 1) for i in range(2 * RINGS)])


def everyone(x):
    own = [x] + [around(x, d) for d in range(1, RINGS)]
    return own + [across(r) for r in own]


def route(x):
    return lax.all_to_all(x, "rows", split_axis=0, concat_axis=0, tiled=True)


def on_device(
    text_embed,
    image_embed,
    image_start,
    norm_gain,
    key_weight,
    value_weight,
    key_target,
    value_target,
):
    shards = lax.axis_size("rows")
    seq_rows = text_embed.shape[0]
    gain = norm_gain[None, :]
    starts = image_start.reshape(shards, -1)

    sent, scaled, lanes, text_held, weight = forward_other(
        text_embed, gain, (key_weight, value_weight)
    )
    arrived = across(sent)
    image_sent, image_scaled, image_lanes, image_held = forward_other(
        image_embed, gain, (weight,)
    )
    image_arrived = across(image_sent)
    goals, target = gather_targets(starts, key_target, value_target)
    own = forward_own(scaled, lanes, weight, arrived)
    parts = [own[0]] + [around(own[d], d) for d in range(1, RINGS)]
    own = forward_own(image_scaled, image_lanes, weight, image_arrived)
    image_parts = [own[0]] + [around(own[d], d) for d in range(1, RINGS)]
    goals, image_parts[0] = lax.optimization_barrier((goals, image_parts[0]))
    goals = route(goals)

    both, resid, inverse = text_combine(parts, target)
    resids = everyone(resid)
    image_send, image_both, image_inverse = image_keys(image_parts, starts, seq_rows)
    landed = route(image_send)
    image_resids = everyone(image_residual(image_both, goals, starts, seq_rows))

    text_grad = backward(text_held, gain, inverse, weight, starts, resids)
    image_grad = backward(image_held, gain, image_inverse, weight, None, image_resids)
    keys, values = merge(starts, landed, both)
    return (keys, values, text_grad, image_grad)


def solution(mesh):
    in_specs = (
        P("rows", "tp"),
        P("rows", "tp"),
        P(),
        P("tp"),
        P("tp", None),
        P("tp", None),
        P("rows", "tp"),
        P("rows", "tp"),
    )
    out_specs = (P("rows", "tp"), P("rows", "tp"), P("rows", "tp"), P("rows", "tp"))
    return jax.shard_map(
        on_device, mesh=mesh, in_specs=in_specs, out_specs=out_specs, check_vma=False
    )
```

```python
import functools

import jax
import jax.numpy as jnp
from jax import lax
from jax.experimental import pallas as pl
from jax.experimental.pallas import tpu as pltpu
from jax.sharding import PartitionSpec as P

WIDTH = 8192
EPSILON = 1e-06
IMAGE_LEN = 24
EXTRA = 16
HEAD = 128
PAIR = 2 * HEAD
RINGS = 4
CHUNKS = 2 * RINGS
PIECE = 128
ABSENT = 8192.0

F32 = jnp.float32
BF16 = jnp.bfloat16
PARAMS = pltpu.CompilerParams(vmem_limit_bytes=24 * 2**20)
IN_VMEM = pl.BlockSpec(memory_space=pltpu.VMEM)
ANYWHERE = pl.BlockSpec(memory_space=pl.ANY)


def near(x):
    return pltpu.with_memory_space_constraint(x, pltpu.VMEM)


def far(x):
    return pltpu.with_memory_space_constraint(x, pltpu.HBM)


def after(x, *others):
    return lax.optimization_barrier((x, *others))[0]


def fetch(pairs, sems, first=0):
    copies = [
        pltpu.make_async_copy(source, target, sems.at[first + n])
        for n, (source, target) in enumerate(pairs)
    ]
    for copy in copies:
        copy.start()
    return copies


def finish(copies):
    for copy in copies:
        copy.wait()


def cost(flops, nbytes):
    return pl.CostEstimate(flops=flops, bytes_accessed=nbytes, transcendentals=0)


def same_index(count):
    shape = (count, count)
    return lax.broadcasted_iota(jnp.int32, shape, 0) == lax.broadcasted_iota(jnp.int32, shape, 1)


def column_to_lanes(column):
    eye = same_index(HEAD)
    row = lax.broadcasted_iota(jnp.int32, (8, HEAD), 0)
    out = jnp.zeros((8, HEAD), F32)
    for p in range(column.shape[0] // HEAD):
        piece = column[p * HEAD : (p + 1) * HEAD, :]
        lanes = jnp.sum(jnp.where(eye, piece, 0.0), axis=0, keepdims=True)
        out = jnp.where(row == p, lanes, out)
    return out


def lanes_to_column(lanes, rows):
    eye = same_index(HEAD)
    pieces = [
        jnp.sum(jnp.where(eye, lanes[p : p + 1, :], 0.0), axis=1, keepdims=True)
        for p in range(rows // HEAD)
    ]
    return jnp.concatenate(pieces, axis=0)


def split_extra(lanes):
    high = lanes.astype(BF16).astype(F32)
    both = jnp.concatenate([high, lanes - high], axis=0)
    return jnp.concatenate([both, jnp.zeros((EXTRA, HEAD), F32)], axis=1).astype(BF16)


def join_extra(block):
    block = block.astype(F32)
    return block[0:8, 0:HEAD] + block[8:16, 0:HEAD]


def my_place():
    mine = lax.axis_index("tp")
    return lax.div(mine, 2), lax.rem(mine, 2)


def head_columns(d, other):
    ring, core = my_place()
    chip = lax.rem(ring + d, RINGS)
    return pl.ds(pl.multiple_of(HEAD * (2 * chip + (1 - core if other else core)), HEAD), HEAD)


def pair_weight(wk_ref, wv_ref, d, other):
    here = head_columns(d, other)
    return jnp.concatenate([wk_ref[:, here], wv_ref[:, here]], axis=1)


def forward_other_kernel(loads, splits, x_ref, gain_ref, *refs):
    from_refs, send_refs, refs = refs[0:2], refs[2 : 2 + len(splits)], refs[2 + len(splits) :]
    if loads:
        wk_from, wv_from = from_refs
        scaled_ref, lanes_ref, wk_ref, wv_ref, held, sems, more = refs
    else:
        wk_ref, wv_ref = from_refs
        scaled_ref, lanes_ref, held, sems = refs
    rows, depth = x_ref.shape[0], wk_ref.shape[0]
    pieces = [pl.ds(p * PIECE, PIECE) for p in range(rows // PIECE)]
    x_copies = fetch([(x_ref.at[p], held.at[p]) for p in pieces], sems)
    weights = []
    if loads:
        spans = [pl.ds(p * PAIR, PAIR) for p in range(depth // PAIR)]
        weights = [(wk_from.at[p], wk_ref.at[p]) for p in spans]
        weights += [(wv_from.at[p], wv_ref.at[p]) for p in spans]
        weights = fetch(weights, more)
    row = lax.broadcasted_iota(jnp.int32, (8, HEAD), 0)
    eye = same_index(HEAD)
    lanes = jnp.zeros((8, HEAD), F32)
    for p, copy in enumerate(x_copies):
        copy.wait()
        here = slice(p * PIECE, (p + 1) * PIECE)
        x = held[here, :].astype(F32)
        scaled_ref[here, :] = (gain_ref[...] * x).astype(BF16)
        squares = jnp.sum(x * x, axis=1, keepdims=True)
        line = jnp.sum(jnp.where(eye, squares, 0.0), axis=0, keepdims=True)
        lanes = jnp.where(row == p, line, lanes)
    lanes_ref[...] = lanes
    extra = split_extra(lanes)
    finish(weights)
    for split, send_ref in zip(splits, send_refs):
        for n, d in enumerate(split):
            weight = pair_weight(wk_ref, wv_ref, d, True)
            product = jnp.dot(scaled_ref[...], weight, preferred_element_type=F32)
            send_ref[n, 0:rows, :] = product.astype(BF16)
            send_ref[n, rows:, :] = extra


def forward_other(x, gain, weights, loads, splits):
    rows, width = x.shape
    out_shape = [pltpu.VMEM((len(split), rows + EXTRA, PAIR), BF16) for split in splits] + [
        pltpu.VMEM(x.shape, BF16),
        pltpu.VMEM((8, HEAD), F32),
    ]
    scratch = [pltpu.VMEM(x.shape, BF16), pltpu.SemaphoreType.DMA((rows // PIECE,))]
    if loads:
        out_shape += [pltpu.VMEM(w.shape, BF16) for w in weights]
        scratch.append(pltpu.SemaphoreType.DMA((2 * width // PAIR,)))
    weights = [far(w) if loads else near(w) for w in weights]
    return pl.pallas_call(
        functools.partial(forward_other_kernel, loads, splits),
        in_specs=[ANYWHERE, IN_VMEM] + [ANYWHERE if loads else IN_VMEM] * 2,
        out_specs=[IN_VMEM] * len(out_shape),
        out_shape=out_shape,
        scratch_shapes=scratch,
        compiler_params=PARAMS,
        cost_estimate=cost(2 * rows * width * RINGS * PAIR, 2**22 if loads else 2**20),
        name="forward_other",
    )(far(x), gain, *weights)


def forward_own_kernel(split, first, close, scaled_ref, lanes_ref, wk_ref, wv_ref, in_ref, *refs):
    out_refs, (held, sems) = refs[0 : len(split)], refs[len(split) :]
    rows = scaled_ref.shape[0]
    extra = split_extra(lanes_ref[...] + join_extra(in_ref[first, rows:, :]))
    copies = []
    for n, d in enumerate(split):
        weight = pair_weight(wk_ref, wv_ref, d, False)
        product = jnp.dot(scaled_ref[...], weight, preferred_element_type=F32)
        total = (product + in_ref[first + n, 0:rows, :].astype(F32)).astype(BF16)
        if d in close:
            out_refs[n][0:rows, :] = total
            out_refs[n][rows:, :] = extra
        else:
            held[n, 0:rows, :] = total
            held[n, rows:, :] = extra
            copies += fetch([(held.at[n], out_refs[n])], sems, n)
    finish(copies)


def forward_own(scaled, lanes, weights, arrived, split, first, close):
    rows, width = scaled.shape
    block = (rows + EXTRA, PAIR)
    sums = pl.pallas_call(
        functools.partial(forward_own_kernel, split, first, close),
        in_specs=[IN_VMEM] * 5,
        out_specs=[IN_VMEM if d in close else ANYWHERE for d in split],
        out_shape=[(pltpu.VMEM if d in close else pltpu.HBM)(block, BF16) for d in split],
        scratch_shapes=[
            pltpu.VMEM((len(split),) + block, BF16),
            pltpu.SemaphoreType.DMA((len(split),)),
        ],
        compiler_params=PARAMS,
        cost_estimate=cost(2 * rows * width * len(split) * PAIR, 2**20),
        name="forward_own",
    )(near(scaled), near(lanes), *[near(w) for w in weights], near(arrived))
    return dict(zip(split, sums))


def gathered(parts):
    rows = parts.shape[1] - EXTRA
    total = parts[0, 0:rows, :].astype(F32)
    lanes = join_extra(parts[0, rows:, :])
    for d in range(1, RINGS):
        total = total + parts[d, 0:rows, :].astype(F32)
        lanes = lanes + join_extra(parts[d, rows:, :])
    inverse = lax.rsqrt(lanes_to_column(lanes, rows) / WIDTH + EPSILON)
    return (inverse * total).astype(BF16), inverse


def residual(both, target, resid_ref):
    rows = both.shape[0]
    both = both.astype(F32)
    resid = (both - target.astype(F32)).astype(BF16)
    dots = jnp.sum(resid.astype(F32) * both, axis=1, keepdims=True)
    resid_ref[0:rows, :] = resid
    resid_ref[rows:, :] = split_extra(column_to_lanes(dots))


def text_combine_kernel(
    a, b, c, d, kt_ref, vt_ref, both_out, resid_out, inverse_out,
    parts, targets, both_ref, resid_ref, inverse_ref, sems,
):
    copies = fetch([(ref, parts.at[n]) for n, ref in enumerate((a, b, c, d))], sems)
    copies += fetch([(kt_ref, targets.at[0]), (vt_ref, targets.at[1])], sems, RINGS)
    finish(copies)
    both, inverse = gathered(parts)
    residual(both, jnp.concatenate([targets[0], targets[1]], axis=1), resid_ref)
    out = fetch([(resid_ref, resid_out)], sems)
    both_ref[...] = both
    inverse_ref[...] = jnp.broadcast_to(inverse, inverse_ref.shape)
    out += fetch([(both_ref, both_out), (inverse_ref, inverse_out)], sems, 1)
    finish(out)


def text_combine(parts, targets):
    rows = targets[0].shape[0]
    shapes = [((rows, PAIR), BF16), (parts[0].shape, BF16), ((rows, HEAD), F32)]
    return pl.pallas_call(
        text_combine_kernel,
        in_specs=[ANYWHERE] * 6,
        out_specs=[ANYWHERE] * 3,
        out_shape=[pltpu.HBM(*s) for s in shapes],
        scratch_shapes=[
            pltpu.VMEM((RINGS,) + parts[0].shape, BF16),
            pltpu.VMEM((2,) + targets[0].shape, BF16),
            *[pltpu.VMEM(*s) for s in shapes],
            pltpu.SemaphoreType.DMA((RINGS + 2,)),
        ],
        compiler_params=PARAMS,
        cost_estimate=cost(2**22, 2**22),
        name="text_combine",
    )(*parts, *[far(t) for t in targets])


def one_hot(match):
    return jnp.where(match, jnp.ones(match.shape, F32), jnp.zeros(match.shape, F32)).astype(BF16)


def slot_columns(rows, first, lanes):
    shape = (rows, lanes.shape[1])
    row = first + lax.broadcasted_iota(jnp.int32, shape, 0)
    begin = IMAGE_LEN * lax.broadcasted_iota(jnp.int32, shape, 1)
    inside = (row >= begin) & (row < begin + IMAGE_LEN)
    value = lanes + (row - begin).astype(F32)
    return jnp.sum(jnp.where(inside, value, 0.0), axis=1, keepdims=True)


def slot_lanes(rows, column):
    shape = (column.shape[0], rows)
    row = lax.broadcasted_iota(jnp.int32, shape, 1)
    begin = IMAGE_LEN * lax.broadcasted_iota(jnp.int32, shape, 0)
    inside = (row >= begin) & (row < begin + IMAGE_LEN)
    value = column + (row - begin).astype(F32)
    return jnp.sum(jnp.where(inside, value, 0.0), axis=0, keepdims=True)


def first_rows(starts_ref, rows):
    shards = lax.axis_size("rows")
    images = starts_ref.shape[1] // shards
    offset = starts_ref[...].astype(F32) - (lax.axis_index("rows") * rows).astype(F32)
    value = jnp.where((offset >= 0.0) & (offset < rows), offset + ABSENT, 0.0)
    shape = (shards, starts_ref.shape[1])
    lane = lax.broadcasted_iota(jnp.int32, shape, 1)
    begin = images * lax.broadcasted_iota(jnp.int32, shape, 0)
    mine = (lane >= begin) & (lane < begin + images)
    column = jnp.sum(jnp.where(mine, value, 0.0), axis=1, keepdims=True) - ABSENT
    return column, jnp.sum(jnp.where(same_index(shards), column, 0.0), axis=0, keepdims=True)


def destinations(starts_ref, rows):
    images = starts_ref.shape[1] // lax.axis_size("rows")
    slot = IMAGE_LEN * jnp.floor((starts_ref[...].astype(F32) + 0.5) / rows)
    shape = (images, starts_ref.shape[1])
    image = lax.axis_index("rows") * images + lax.broadcasted_iota(jnp.int32, shape, 0)
    mine = lax.broadcasted_iota(jnp.int32, shape, 1) == image
    column = jnp.sum(jnp.where(mine, slot, 0.0), axis=1, keepdims=True)
    return jnp.sum(jnp.where(same_index(images), column, 0.0), axis=0, keepdims=True), column


def image_keys_kernel(
    seq_rows, a, b, c, d, starts_ref, send_out, both_out, inverse_out,
    parts, send_ref, both_ref, inverse_ref, sems,
):
    copies = fetch([(ref, parts.at[n]) for n, ref in enumerate((a, b, c, d))], sems)
    rows, slots = both_ref.shape[0], send_ref.shape[0]
    _, dest = destinations(starts_ref, seq_rows)
    slot = lax.broadcasted_iota(jnp.int32, (slots, rows), 0).astype(F32)
    picks = one_hot(slot == slot_lanes(rows, dest))
    finish(copies)
    both, inverse = gathered(parts)
    send_ref[...] = jnp.dot(picks, both, preferred_element_type=F32).astype(BF16)
    out = fetch([(send_ref, send_out)], sems)
    both_ref[...] = both
    inverse_ref[...] = jnp.broadcast_to(inverse, inverse_ref.shape)
    out += fetch([(both_ref, both_out), (inverse_ref, inverse_out)], sems, 1)
    finish(out)


def image_keys(parts, starts, seq_rows):
    rows = parts[0].shape[0] - EXTRA
    slots = lax.axis_size("rows") * IMAGE_LEN
    shapes = [((slots, PAIR), BF16), ((rows, PAIR), BF16), ((rows, HEAD), F32)]
    return pl.pallas_call(
        functools.partial(image_keys_kernel, seq_rows),
        in_specs=[ANYWHERE] * RINGS + [IN_VMEM],
        out_specs=[ANYWHERE] * 3,
        out_shape=[pltpu.HBM(*s) for s in shapes],
        scratch_shapes=[
            pltpu.VMEM((RINGS,) + parts[0].shape, BF16),
            *[pltpu.VMEM(*s) for s in shapes],
            pltpu.SemaphoreType.DMA((RINGS,)),
        ],
        compiler_params=PARAMS,
        cost_estimate=cost(2**28, 2**20),
        name="image_keys",
    )(*parts, starts)


def image_residual_kernel(
    seq_rows, both_from, arrived_from, starts_ref, resid_out, both_ref, arrived_ref, resid_ref, sems
):
    copies = fetch([(both_from, both_ref), (arrived_from, arrived_ref)], sems)
    rows = both_ref.shape[0]
    dest, _ = destinations(starts_ref, seq_rows)
    shape = (rows, arrived_ref.shape[0])
    slot = lax.broadcasted_iota(jnp.int32, shape, 1).astype(F32)
    picks = one_hot(slot == slot_columns(rows, 0, dest))
    finish(copies)
    target = jnp.dot(picks, arrived_ref[...], preferred_element_type=F32)
    residual(both_ref[...], target, resid_ref)
    finish(fetch([(resid_ref, resid_out)], sems))


def image_residual(both, arrived, starts, seq_rows):
    shape = (both.shape[0] + EXTRA, PAIR)
    return pl.pallas_call(
        functools.partial(image_residual_kernel, seq_rows),
        in_specs=[ANYWHERE, ANYWHERE, IN_VMEM],
        out_specs=ANYWHERE,
        out_shape=pltpu.HBM(shape, BF16),
        scratch_shapes=[
            pltpu.VMEM(both.shape, BF16),
            pltpu.VMEM(arrived.shape, BF16),
            pltpu.VMEM(shape, BF16),
            pltpu.SemaphoreType.DMA((2,)),
        ],
        compiler_params=PARAMS,
        cost_estimate=cost(2**28, 2**20),
        name="image_residual",
    )(both, arrived, starts)


def gather_kernel(starts_ref, kt_from, vt_from, out_ref, halves, target_ref, held, sems):
    copies = fetch([(kt_from, halves.at[0]), (vt_from, halves.at[1])], sems)
    rows = target_ref.shape[0]
    _, first = first_rows(starts_ref, rows)
    finish(copies)
    target_ref[:, 0:HEAD] = halves[0]
    target_ref[:, HEAD:] = halves[1]
    for begin in range(0, out_ref.shape[0], PAIR):
        place = slot_columns(PAIR, begin, first)
        position = lax.broadcasted_iota(jnp.int32, (PAIR, rows), 1).astype(F32)
        picked = jnp.dot(
            one_hot(position == place), target_ref[...], preferred_element_type=F32
        )
        held[begin : begin + PAIR, :] = picked.astype(BF16)
    finish(fetch([(held, out_ref)], sems))


def gather_targets(starts, key_target, value_target):
    shape = (lax.axis_size("rows") * IMAGE_LEN, PAIR)
    return pl.pallas_call(
        gather_kernel,
        in_specs=[IN_VMEM, ANYWHERE, ANYWHERE],
        out_specs=ANYWHERE,
        out_shape=pltpu.HBM(shape, BF16),
        scratch_shapes=[
            pltpu.VMEM((2,) + key_target.shape, BF16),
            pltpu.VMEM((key_target.shape[0], PAIR), BF16),
            pltpu.VMEM(shape, BF16),
            pltpu.SemaphoreType.DMA((2,)),
        ],
        compiler_params=PARAMS,
        cost_estimate=cost(2**28, 2**20),
        name="gather_targets",
    )(starts, far(key_target), far(value_target))


def image_rows_mask(rows, first_row, first_lanes):
    shape = (rows, first_lanes.shape[1])
    row = (first_row + lax.broadcasted_iota(jnp.int32, shape, 0)).astype(F32)
    inside = (row >= first_lanes) & (row < first_lanes + IMAGE_LEN)
    return jnp.sum(jnp.where(inside, 1.0, 0.0), axis=1, keepdims=True) > 0.5


def merge_kernel(
    starts_ref, arrived_from, both_from, keys_out, values_out,
    arrived_ref, both_ref, keys_ref, values_ref, sems,
):
    copies = fetch([(arrived_from, arrived_ref), (both_from, both_ref)], sems)
    slots, rows = arrived_ref.shape[0], both_ref.shape[0]
    column, lanes = first_rows(starts_ref, rows)
    place = slot_lanes(slots, column)
    finish(copies)
    for begin in range(0, rows, PAIR):
        row = begin + lax.broadcasted_iota(jnp.int32, (PAIR, slots), 0)
        picks = one_hot(row.astype(F32) == place)
        landed = jnp.dot(picks, arrived_ref[...], preferred_element_type=F32)
        here = slice(begin, begin + PAIR)
        mask = image_rows_mask(PAIR, begin, lanes)
        both = jnp.where(mask, landed, both_ref[here, :].astype(F32)).astype(BF16)
        keys_ref[here, :] = both[:, 0:HEAD]
        values_ref[here, :] = both[:, HEAD:]
    finish(fetch([(keys_ref, keys_out), (values_ref, values_out)], sems))


def merge(starts, arrived, both):
    shape = (both.shape[0], HEAD)
    return pl.pallas_call(
        merge_kernel,
        in_specs=[IN_VMEM, ANYWHERE, ANYWHERE],
        out_specs=[ANYWHERE] * 2,
        out_shape=[jax.ShapeDtypeStruct(shape, BF16)] * 2,
        scratch_shapes=[
            pltpu.VMEM(arrived.shape, BF16),
            pltpu.VMEM(both.shape, BF16),
            pltpu.VMEM(shape, BF16),
            pltpu.VMEM(shape, BF16),
            pltpu.SemaphoreType.DMA((2,)),
        ],
        compiler_params=PARAMS,
        cost_estimate=cost(2**28, 2**20),
        name="merge",
    )(starts, arrived, both)


def stack_parts(resids, parts, stacked, sems):
    rows = stacked.shape[0]
    copies = fetch([(ref, parts.at[n]) for n, ref in enumerate(resids)], sems)
    lanes = jnp.zeros((8, HEAD), F32)
    for n, copy in enumerate(copies):
        copy.wait()
        stacked[:, n * PAIR : (n + 1) * PAIR] = parts[n, 0:rows, :]
        lanes = lanes + join_extra(parts[n, rows:, :])
    return lanes


def tile_product(stacked, wk_ref, wv_ref, here, other):
    pieces = []
    for n in range(RINGS):
        columns = head_columns((RINGS - n) % RINGS, other)
        pieces += [wk_ref[here, columns], wv_ref[here, columns]]
    contract = (((1,), (1,)), ((), ()))
    weight = jnp.concatenate(pieces, axis=1)
    return lax.dot_general(stacked[...], weight, contract, preferred_element_type=F32)


TILE = 256


def backward_own_kernel(loads, *refs):
    froms, resids, refs = refs[0:2], refs[2 : 2 + RINGS], refs[2 + RINGS :]
    if loads:
        total_ref, lanes_ref, wk_ref, wv_ref, parts, stacked, sems, more = refs
    else:
        wk_ref, wv_ref = froms
        total_ref, lanes_ref, parts, stacked, sems = refs
    tiles = total_ref.shape[1] // TILE
    weights = []
    for n in range(tiles if loads else 0):
        span = pl.ds(n * TILE, TILE)
        pairs = zip(froms, (wk_ref, wv_ref))
        weights.append(fetch([(source.at[span], to.at[span]) for source, to in pairs], more, 2 * n))
    lanes_ref[...] = stack_parts(resids, parts, stacked, sems)
    for n in range(tiles):
        here = slice(n * TILE, (n + 1) * TILE)
        finish(weights[n] if loads else [])
        total_ref[:, here] = tile_product(stacked, wk_ref, wv_ref, here, False)


def backward_own(weights, resids, rows, loads):
    width = weights[0].shape[0]
    out_shape = [pltpu.VMEM((rows, width), F32), pltpu.VMEM((8, HEAD), F32)]
    scratch = [
        pltpu.VMEM((RINGS,) + resids[0].shape, BF16),
        pltpu.VMEM((rows, RINGS * PAIR), BF16),
        pltpu.SemaphoreType.DMA((RINGS,)),
    ]
    if loads:
        out_shape += [pltpu.VMEM(w.shape, BF16) for w in weights]
        scratch.append(pltpu.SemaphoreType.DMA((2 * width // TILE,)))
    return pl.pallas_call(
        functools.partial(backward_own_kernel, loads),
        in_specs=[ANYWHERE if loads else IN_VMEM] * 2 + [ANYWHERE] * RINGS,
        out_specs=[IN_VMEM] * len(out_shape),
        out_shape=out_shape,
        scratch_shapes=scratch,
        compiler_params=PARAMS,
        cost_estimate=cost(2 * rows * width * RINGS * PAIR, 2**21),
        name="backward_own",
    )(*[far(w) if loads else near(w) for w in weights], *resids)


def backward_other_kernel(
    masked, x_from, gain_ref, starts_ref, inverse_from, wk_ref, wv_ref, total_ref, lanes_ref, *rest
):
    resids, rest = rest[0:RINGS], rest[RINGS:]
    out_ref, parts, stacked, inverse_ref, x_ref, held, sems = rest
    rows, width = x_ref.shape
    late = [(inverse_from, inverse_ref), (x_from, x_ref)]
    if masked:
        mask = image_rows_mask(rows, 0, first_rows(starts_ref, rows)[1])
    late = fetch(late, sems, RINGS)
    lanes = lanes_ref[...] + stack_parts(resids, parts, stacked, sems)
    finish(late)
    inverse = inverse_ref[:, 0:1]
    coefficient = inverse * inverse * lanes_to_column(lanes, rows) / WIDTH
    out = []
    for n in range(width // TILE):
        here = slice(n * TILE, (n + 1) * TILE)
        back = total_ref[:, here] + tile_product(stacked, wk_ref, wv_ref, here, True)
        grad = gain_ref[:, here] * inverse * back - coefficient * x_ref[:, here].astype(F32)
        if masked:
            grad = jnp.where(mask, 0.0, grad)
        held[:, here] = grad.astype(BF16)
        span = pl.ds(n * TILE, TILE)
        out += fetch([(held.at[:, span], out_ref.at[:, span])], sems, n)
    finish(out)


def backward_other(x, gain, inverse, weights, starts, before, resids, masked):
    rows, width = x.shape
    return pl.pallas_call(
        functools.partial(backward_other_kernel, masked),
        in_specs=[ANYWHERE] + [IN_VMEM] * 2 + [ANYWHERE] + [IN_VMEM] * 4 + [ANYWHERE] * RINGS,
        out_specs=ANYWHERE,
        out_shape=jax.ShapeDtypeStruct(x.shape, BF16),
        scratch_shapes=[
            pltpu.VMEM((RINGS,) + resids[0].shape, BF16),
            pltpu.VMEM((rows, RINGS * PAIR), BF16),
            pltpu.VMEM((rows, HEAD), F32),
            pltpu.VMEM(x.shape, BF16),
            pltpu.VMEM(x.shape, BF16),
            pltpu.SemaphoreType.DMA((RINGS + 2,)),
        ],
        compiler_params=PARAMS,
        cost_estimate=cost(2 * rows * width * RINGS * PAIR, 2**21),
        name="backward_other",
    )(far(x), gain, starts, inverse, *[near(w) for w in weights], *[near(b) for b in before], *resids)


def around(x, shift):
    return lax.ppermute(
        x, "tp", [(2 * y + c, 2 * ((y + shift) % RINGS) + c) for y in range(RINGS) for c in range(2)]
    )


def across(x):
    return lax.ppermute(x, "tp", [(i, i ^ 1) for i in range(2 * RINGS)])


def route(x):
    return lax.all_to_all(x, "rows", split_axis=0, concat_axis=0, tiled=True)


def on_device(
    text_embed,
    image_embed,
    image_start,
    norm_gain,
    key_weight,
    value_weight,
    key_target,
    value_target,
):
    seq_rows = text_embed.shape[0]
    gain = norm_gain[None, :]
    starts = image_start[None, :]
    weights = (key_weight, value_weight)
    targets = (key_target, value_target)

    early, late = (2, 1), (3, 0)
    sent_early, sent_late, scaled, lanes, *held = forward_other(
        text_embed, gain, weights, True, (early, late)
    )
    arrived_early, arrived_late = across(sent_early), across(sent_late)
    image_sent, image_scaled, image_lanes = forward_other(
        image_embed, gain, held, False, (early + late,)
    )
    image_arrived = across(image_sent)
    close = (2, 1, 3)
    sums = forward_own(after(scaled, image_sent), lanes, held, arrived_early, early, 0, close)
    sums |= forward_own(after(scaled, sums[1]), lanes, held, arrived_late, late, 0, close)
    part2, part1, part3 = [around(sums[d], d) for d in (2, 1, 3)]
    image_sums = forward_own(
        after(image_scaled, sums[0]), image_lanes, held, image_arrived, early, 0, ()
    )
    image2 = around(image_sums[2], 2)
    image_sums |= forward_own(
        after(image_scaled, image_sums[1]), image_lanes, held, image_arrived, late, 2, ()
    )
    goals = route(gather_targets(after(starts, image_sums[0]), *targets))
    image1 = around(after(image_sums[1], part1), 1)
    image3 = around(after(image_sums[3], part3), 3)

    both, resid, inverse = text_combine((sums[0], part1, part2, part3), targets)
    resid2 = around(after(resid, image2), 2)
    resid1 = around(after(resid, image1), 1)
    resid3 = around(after(resid, image3), 3)
    image_send, image_both, image_inverse = image_keys(
        (after(image_sums[0], resid), image1, image2, image3), starts, seq_rows
    )
    landed = route(image_send)
    image_resid = image_residual(image_both, goals, starts, seq_rows)
    image_resid2 = around(image_resid, 2)
    image_resid1 = around(after(image_resid, resid1), 1)
    image_resid3 = around(after(image_resid, resid3), 3)

    own = [resid, resid1, resid2, resid3]
    other = [across(r) for r in own]
    *before, wk, wv = backward_own(weights, own, seq_rows, True)
    held = (wk, wv)
    text_grad = backward_other(text_embed, gain, inverse, held, starts, before, other, True)
    own = [after(image_resid, text_grad), image_resid1, image_resid2, image_resid3]
    other = [across(r) for r in own]
    before = backward_own(held, own, image_embed.shape[0], False)
    image_grad = backward_other(
        image_embed, gain, image_inverse, held, starts, before, other, False
    )
    keys, values = merge(after(starts, image_grad), landed, both)
    return (keys, values, text_grad, image_grad)


def solution(mesh):
    in_specs = (
        P("rows", "tp"),
        P("rows", "tp"),
        P(),
        P("tp"),
        P("tp", None),
        P("tp", None),
        P("rows", "tp"),
        P("rows", "tp"),
    )
    out_specs = (P("rows", "tp"), P("rows", "tp"), P("rows", "tp"), P("rows", "tp"))
    return jax.shard_map(
        on_device, mesh=mesh, in_specs=in_specs, out_specs=out_specs, check_vma=False
    )
```

```python
import functools

import jax
import jax.numpy as jnp
from jax import lax
from jax.experimental import pallas as pl
from jax.experimental.pallas import tpu as pltpu
from jax.sharding import PartitionSpec as P

WIDTH = 8192
EPSILON = 1e-06
IMAGE_LEN = 24
EXTRA = 16
HEAD = 128
PAIR = 2 * HEAD
RINGS = 4
CHUNKS = 2 * RINGS
PIECE = 128
ABSENT = 8192.0

F32 = jnp.float32
BF16 = jnp.bfloat16
PARAMS = pltpu.CompilerParams(vmem_limit_bytes=24 * 2**20)
IN_VMEM = pl.BlockSpec(memory_space=pltpu.VMEM)
ANYWHERE = pl.BlockSpec(memory_space=pl.ANY)


def near(x):
    return pltpu.with_memory_space_constraint(x, pltpu.VMEM)


def far(x):
    return pltpu.with_memory_space_constraint(x, pltpu.HBM)


def after(x, *others):
    return lax.optimization_barrier((x, *others))[0]


def fetch(pairs, sems, first=0):
    copies = [
        pltpu.make_async_copy(source, target, sems.at[first + n])
        for n, (source, target) in enumerate(pairs)
    ]
    for copy in copies:
        copy.start()
    return copies


def finish(copies):
    for copy in copies:
        copy.wait()


SMALL = pl.CostEstimate(flops=2**20, bytes_accessed=2**16, transcendentals=0)


def same_index(count):
    shape = (count, count)
    return lax.broadcasted_iota(jnp.int32, shape, 0) == lax.broadcasted_iota(jnp.int32, shape, 1)


def with_piece(lanes, p, column):
    line = jnp.sum(jnp.where(same_index(HEAD), column, 0.0), axis=0, keepdims=True)
    return jnp.where(lax.broadcasted_iota(jnp.int32, lanes.shape, 0) == p, line, lanes)


def with_column(lanes, column, first=0):
    for p in range(column.shape[0] // HEAD):
        lanes = with_piece(lanes, first + p, column[p * HEAD : (p + 1) * HEAD, :])
    return lanes


def lanes_to_column(lanes, first, rows):
    eye = same_index(HEAD)
    pieces = [
        jnp.sum(jnp.where(eye, lanes[p : p + 1, :], 0.0), axis=1, keepdims=True)
        for p in range(first, first + rows // HEAD)
    ]
    return jnp.concatenate(pieces, axis=0)


def no_lanes():
    return jnp.zeros((EXTRA, HEAD), F32)


def split_extra(lanes):
    high = lanes.astype(BF16).astype(F32)
    return jnp.concatenate([high, lanes - high], axis=1).astype(BF16)


def join_extra(block):
    block = block.astype(F32)
    return block[:, 0:HEAD] + block[:, HEAD:]


def my_place():
    mine = lax.axis_index("tp")
    return lax.div(mine, 2), lax.rem(mine, 2)


def head_columns(d, other):
    ring, core = my_place()
    chip = lax.rem(ring + d, RINGS)
    return pl.ds(pl.multiple_of(HEAD * (2 * chip + (1 - core if other else core)), HEAD), HEAD)


def pair_weight(wk_ref, wv_ref, d, other):
    here = head_columns(d, other)
    return jnp.concatenate([wk_ref[:, here], wv_ref[:, here]], axis=1)


def forward_other_kernel(
    splits, text_ref, image_ref, gain_ref, wk_from, wv_from,
    early_ref, late_ref, scaled_ref, lanes_ref, wk_ref, wv_ref, held, sems, more,
):
    rows, depth = scaled_ref.shape
    pairs = []
    for ref in (text_ref, image_ref):
        for p in range(ref.shape[0] // PIECE):
            to = held.at[pl.ds(len(pairs) * PIECE, PIECE)]
            pairs.append((ref.at[pl.ds(p * PIECE, PIECE)], to))
    x_copies = fetch(pairs, sems)
    spans = [pl.ds(p * PAIR, PAIR) for p in range(depth // PAIR)]
    weights = [(wk_from.at[p], wk_ref.at[p]) for p in spans]
    weights += [(wv_from.at[p], wv_ref.at[p]) for p in spans]
    weights = fetch(weights, more)
    lanes = no_lanes()
    for p, copy in enumerate(x_copies):
        copy.wait()
        here = slice(p * PIECE, (p + 1) * PIECE)
        x = held[here, :].astype(F32)
        scaled_ref[here, :] = (gain_ref[...] * x).astype(BF16)
        lanes = with_piece(lanes, p, jnp.sum(x * x, axis=1, keepdims=True))
    lanes_ref[...] = lanes
    extra = split_extra(lanes)
    finish(weights)
    for split, send_ref in zip(splits, (early_ref, late_ref)):
        for n, d in enumerate(split):
            weight = pair_weight(wk_ref, wv_ref, d, True)
            product = jnp.dot(scaled_ref[...], weight, preferred_element_type=F32)
            send_ref[n, 0:rows, :] = product.astype(BF16)
            send_ref[n, rows:, :] = extra


def forward_other(text, image, gain, weights, splits):
    rows, width = text.shape[0] + image.shape[0], text.shape[1]
    out_shape = [pltpu.VMEM((len(split), rows + EXTRA, PAIR), BF16) for split in splits] + [
        pltpu.VMEM((rows, width), BF16),
        pltpu.VMEM((EXTRA, HEAD), F32),
    ]
    out_shape += [pltpu.VMEM(w.shape, BF16) for w in weights]
    return pl.pallas_call(
        functools.partial(forward_other_kernel, splits),
        in_specs=[ANYWHERE, ANYWHERE, IN_VMEM, ANYWHERE, ANYWHERE],
        out_specs=[IN_VMEM] * len(out_shape),
        out_shape=out_shape,
        scratch_shapes=[
            pltpu.VMEM((rows, width), BF16),
            pltpu.SemaphoreType.DMA((rows // PIECE,)),
            pltpu.SemaphoreType.DMA((2 * width // PAIR,)),
        ],
        compiler_params=PARAMS,
        cost_estimate=SMALL,
        name="forward_other",
    )(far(text), far(image), gain, *[far(w) for w in weights])


def forward_own_kernel(split, close, scaled_ref, lanes_ref, wk_ref, wv_ref, in_ref, *refs):
    out_refs, (held, sems) = refs[0 : len(split)], refs[len(split) :]
    rows = scaled_ref.shape[0]
    extra = split_extra(lanes_ref[...] + join_extra(in_ref[0, rows:, :]))
    copies = []
    for n, d in enumerate(split):
        weight = pair_weight(wk_ref, wv_ref, d, False)
        product = jnp.dot(scaled_ref[...], weight, preferred_element_type=F32)
        total = (product + in_ref[n, 0:rows, :].astype(F32)).astype(BF16)
        if d in close:
            out_refs[n][0:rows, :] = total
            out_refs[n][rows:, :] = extra
        else:
            held[n, 0:rows, :] = total
            held[n, rows:, :] = extra
            copies += fetch([(held.at[n], out_refs[n])], sems, n)
    finish(copies)


def forward_own(scaled, lanes, weights, arrived, split, close):
    rows, width = scaled.shape
    block = (rows + EXTRA, PAIR)
    sums = pl.pallas_call(
        functools.partial(forward_own_kernel, split, close),
        in_specs=[IN_VMEM] * 5,
        out_specs=[IN_VMEM if d in close else ANYWHERE for d in split],
        out_shape=[(pltpu.VMEM if d in close else pltpu.HBM)(block, BF16) for d in split],
        scratch_shapes=[
            pltpu.VMEM((len(split),) + block, BF16),
            pltpu.SemaphoreType.DMA((len(split),)),
        ],
        compiler_params=PARAMS,
        cost_estimate=SMALL,
        name="forward_own",
    )(near(scaled), near(lanes), *[near(w) for w in weights], near(arrived))
    return dict(zip(split, sums))


def inverse_of(squares, first, rows):
    return lax.rsqrt(lanes_to_column(squares, first, rows) / WIDTH + EPSILON)


def total_of(parts):
    total = parts[0].astype(F32)
    for d in range(1, RINGS):
        total = total + parts[d].astype(F32)
    return total


def residual(both, target):
    both = both.astype(F32)
    resid = (both - target.astype(F32)).astype(BF16)
    return resid, jnp.sum(resid.astype(F32) * both, axis=1, keepdims=True)


def text_combine_kernel(
    a, b, c, d, kt_ref, vt_ref, both_out, resid_out, squares_ref,
    parts, extras, targets, both_ref, resid_ref, sems, more, stores,
):
    rows, all_rows = both_ref.shape[0], a.shape[0] - EXTRA
    step = PAIR
    tail = pl.ds(all_rows, EXTRA)
    spare = fetch([(ref.at[tail], extras.at[n]) for n, ref in enumerate((a, b, c, d))], more)
    loads = []
    for begin in range(0, rows, step):
        span = pl.ds(begin, step)
        pairs = [(ref.at[span], parts.at[n, span]) for n, ref in enumerate((a, b, c, d))]
        pairs += [(ref.at[span], targets.at[n, span]) for n, ref in enumerate((kt_ref, vt_ref))]
        loads.append(fetch(pairs, sems, len(loads) * (RINGS + 2)))
    finish(spare)
    squares = total_of([join_extra(extras[n]) for n in range(RINGS)])
    squares_ref[...] = squares
    lanes, out = no_lanes(), []
    for n, begin in enumerate(range(0, rows, step)):
        here, span = slice(begin, begin + step), pl.ds(begin, step)
        inverse = inverse_of(squares, begin // HEAD, step)
        finish(loads[n])
        total = total_of([parts[m, here, :] for m in range(RINGS)])
        both = (inverse * total).astype(BF16)
        target = jnp.concatenate([targets[0, here, :], targets[1, here, :]], axis=1)
        resid, dots = residual(both, target)
        resid_ref[here, :] = resid
        both_ref[here, :] = both
        pairs = [(resid_ref.at[span], resid_out.at[span]), (both_ref.at[span], both_out.at[span])]
        out += fetch(pairs, stores, 2 * n)
        lanes = with_column(lanes, dots, begin // HEAD)
    resid_ref[rows:, :] = split_extra(lanes)
    tail = pl.ds(rows, EXTRA)
    out += fetch([(resid_ref.at[tail], resid_out.at[tail])], stores, len(out))
    finish(out)


def text_combine(parts, targets):
    rows = targets[0].shape[0]
    shapes = [((rows, PAIR), BF16), ((rows + EXTRA, PAIR), BF16)]
    steps = rows // PAIR
    return pl.pallas_call(
        text_combine_kernel,
        in_specs=[ANYWHERE] * 6,
        out_specs=[ANYWHERE] * 2 + [IN_VMEM],
        out_shape=[*[pltpu.HBM(*s) for s in shapes], jax.ShapeDtypeStruct((EXTRA, HEAD), F32)],
        scratch_shapes=[
            pltpu.VMEM((RINGS, rows, PAIR), BF16),
            pltpu.VMEM((RINGS, EXTRA, PAIR), BF16),
            pltpu.VMEM((2,) + targets[0].shape, BF16),
            *[pltpu.VMEM(*s) for s in shapes],
            pltpu.SemaphoreType.DMA((steps * (RINGS + 2),)),
            pltpu.SemaphoreType.DMA((RINGS,)),
            pltpu.SemaphoreType.DMA((2 * steps + 1,)),
        ],
        compiler_params=PARAMS,
        cost_estimate=SMALL,
        name="text_combine",
    )(far(parts[0]), *parts[1:], *[far(t) for t in targets])


def one_hot(match):
    return jnp.where(match, jnp.ones(match.shape, F32), jnp.zeros(match.shape, F32)).astype(BF16)


def slot_columns(rows, first, lanes):
    shape = (rows, lanes.shape[1])
    row = first + lax.broadcasted_iota(jnp.int32, shape, 0)
    begin = IMAGE_LEN * lax.broadcasted_iota(jnp.int32, shape, 1)
    inside = (row >= begin) & (row < begin + IMAGE_LEN)
    value = lanes + (row - begin).astype(F32)
    return jnp.sum(jnp.where(inside, value, 0.0), axis=1, keepdims=True)


def slot_lanes(rows, column):
    shape = (column.shape[0], rows)
    row = lax.broadcasted_iota(jnp.int32, shape, 1)
    begin = IMAGE_LEN * lax.broadcasted_iota(jnp.int32, shape, 0)
    inside = (row >= begin) & (row < begin + IMAGE_LEN)
    value = column + (row - begin).astype(F32)
    return jnp.sum(jnp.where(inside, value, 0.0), axis=0, keepdims=True)


def first_rows(starts_ref, rows):
    shards = lax.axis_size("rows")
    images = starts_ref.shape[1] // shards
    offset = starts_ref[...].astype(F32) - (lax.axis_index("rows") * rows).astype(F32)
    value = jnp.where((offset >= 0.0) & (offset < rows), offset + ABSENT, 0.0)
    shape = (shards, starts_ref.shape[1])
    lane = lax.broadcasted_iota(jnp.int32, shape, 1)
    begin = images * lax.broadcasted_iota(jnp.int32, shape, 0)
    mine = (lane >= begin) & (lane < begin + images)
    column = jnp.sum(jnp.where(mine, value, 0.0), axis=1, keepdims=True) - ABSENT
    return column, jnp.sum(jnp.where(same_index(shards), column, 0.0), axis=0, keepdims=True)


def destinations(starts_ref, rows):
    images = starts_ref.shape[1] // lax.axis_size("rows")
    slot = IMAGE_LEN * jnp.floor((starts_ref[...].astype(F32) + 0.5) / rows)
    shape = (images, starts_ref.shape[1])
    image = lax.axis_index("rows") * images + lax.broadcasted_iota(jnp.int32, shape, 0)
    mine = lax.broadcasted_iota(jnp.int32, shape, 1) == image
    column = jnp.sum(jnp.where(mine, slot, 0.0), axis=1, keepdims=True)
    return jnp.sum(jnp.where(same_index(images), column, 0.0), axis=0, keepdims=True), column


def image_keys_kernel(
    seq_rows, a, b, c, d, starts_ref, squares_ref, send_out, both_out,
    parts, send_ref, both_ref, sems,
):
    rows, slots = both_ref.shape[0], send_ref.shape[0]
    span = pl.ds(seq_rows, rows)
    copies = fetch([(ref.at[span], parts.at[n]) for n, ref in enumerate((a, b, c, d))], sems)
    _, dest = destinations(starts_ref, seq_rows)
    slot = lax.broadcasted_iota(jnp.int32, (slots, rows), 0).astype(F32)
    picks = one_hot(slot == slot_lanes(rows, dest))
    inverse = inverse_of(squares_ref[...], seq_rows // HEAD, rows)
    finish(copies)
    both = (inverse * total_of([parts[n] for n in range(RINGS)])).astype(BF16)
    both_ref[...] = both
    out = fetch([(both_ref, both_out)], sems)
    send_ref[...] = jnp.dot(picks, both, preferred_element_type=F32).astype(BF16)
    out += fetch([(send_ref, send_out)], sems, 1)
    finish(out)


def image_keys(parts, starts, squares, rows, seq_rows):
    slots = lax.axis_size("rows") * IMAGE_LEN
    shapes = [((slots, PAIR), BF16), ((rows, PAIR), BF16)]
    return pl.pallas_call(
        functools.partial(image_keys_kernel, seq_rows),
        in_specs=[ANYWHERE] * RINGS + [IN_VMEM] * 2,
        out_specs=[ANYWHERE] * 2,
        out_shape=[pltpu.HBM(*s) for s in shapes],
        scratch_shapes=[
            pltpu.VMEM((RINGS, rows, PAIR), BF16),
            *[pltpu.VMEM(*s) for s in shapes],
            pltpu.SemaphoreType.DMA((RINGS,)),
        ],
        compiler_params=PARAMS,
        cost_estimate=SMALL,
        name="image_keys",
    )(far(parts[0]), *parts[1:], starts, squares)


def image_residual_kernel(
    seq_rows, both_from, arrived_from, starts_ref, resid_out, both_ref, arrived_ref, resid_ref, sems
):
    copies = fetch([(both_from, both_ref), (arrived_from, arrived_ref)], sems)
    rows = both_ref.shape[0]
    dest, _ = destinations(starts_ref, seq_rows)
    shape = (rows, arrived_ref.shape[0])
    slot = lax.broadcasted_iota(jnp.int32, shape, 1).astype(F32)
    picks = one_hot(slot == slot_columns(rows, 0, dest))
    finish(copies)
    target = jnp.dot(picks, arrived_ref[...], preferred_element_type=F32)
    resid, dots = residual(both_ref[...], target)
    resid_ref[0:rows, :] = resid
    resid_ref[rows:, :] = split_extra(with_column(no_lanes(), dots))
    finish(fetch([(resid_ref, resid_out)], sems))


def image_residual(both, arrived, starts, seq_rows):
    shape = (both.shape[0] + EXTRA, PAIR)
    return pl.pallas_call(
        functools.partial(image_residual_kernel, seq_rows),
        in_specs=[ANYWHERE, ANYWHERE, IN_VMEM],
        out_specs=ANYWHERE,
        out_shape=pltpu.HBM(shape, BF16),
        scratch_shapes=[
            pltpu.VMEM(both.shape, BF16),
            pltpu.VMEM(arrived.shape, BF16),
            pltpu.VMEM(shape, BF16),
            pltpu.SemaphoreType.DMA((2,)),
        ],
        compiler_params=PARAMS,
        cost_estimate=SMALL,
        name="image_residual",
    )(far(both), arrived, starts)


def gather_kernel(starts_ref, kt_from, vt_from, out_ref, halves, target_ref, held, sems):
    copies = fetch([(kt_from, halves.at[0]), (vt_from, halves.at[1])], sems)
    rows = target_ref.shape[0]
    _, first = first_rows(starts_ref, rows)
    finish(copies)
    target_ref[:, 0:HEAD] = halves[0]
    target_ref[:, HEAD:] = halves[1]
    for begin in range(0, out_ref.shape[0], PAIR):
        place = slot_columns(PAIR, begin, first)
        position = lax.broadcasted_iota(jnp.int32, (PAIR, rows), 1).astype(F32)
        picked = jnp.dot(
            one_hot(position == place), target_ref[...], preferred_element_type=F32
        )
        held[begin : begin + PAIR, :] = picked.astype(BF16)
    finish(fetch([(held, out_ref)], sems))


def gather_targets(starts, key_target, value_target):
    shape = (lax.axis_size("rows") * IMAGE_LEN, PAIR)
    return pl.pallas_call(
        gather_kernel,
        in_specs=[IN_VMEM, ANYWHERE, ANYWHERE],
        out_specs=ANYWHERE,
        out_shape=pltpu.HBM(shape, BF16),
        scratch_shapes=[
            pltpu.VMEM((2,) + key_target.shape, BF16),
            pltpu.VMEM((key_target.shape[0], PAIR), BF16),
            pltpu.VMEM(shape, BF16),
            pltpu.SemaphoreType.DMA((2,)),
        ],
        compiler_params=PARAMS,
        cost_estimate=SMALL,
        name="gather_targets",
    )(starts, far(key_target), far(value_target))


def image_rows_mask(rows, first_row, first_lanes):
    shape = (rows, first_lanes.shape[1])
    row = (first_row + lax.broadcasted_iota(jnp.int32, shape, 0)).astype(F32)
    inside = (row >= first_lanes) & (row < first_lanes + IMAGE_LEN)
    return jnp.sum(jnp.where(inside, 1.0, 0.0), axis=1, keepdims=True) > 0.5


def merge_kernel(
    starts_ref, arrived_from, both_from, keys_out, values_out,
    arrived_ref, both_ref, keys_ref, values_ref, sems,
):
    copies = fetch([(arrived_from, arrived_ref), (both_from, both_ref)], sems)
    slots, rows = arrived_ref.shape[0], both_ref.shape[0]
    column, lanes = first_rows(starts_ref, rows)
    place = slot_lanes(slots, column)
    finish(copies)
    for begin in range(0, rows, PAIR):
        row = begin + lax.broadcasted_iota(jnp.int32, (PAIR, slots), 0)
        picks = one_hot(row.astype(F32) == place)
        landed = jnp.dot(picks, arrived_ref[...], preferred_element_type=F32)
        here = slice(begin, begin + PAIR)
        mask = image_rows_mask(PAIR, begin, lanes)
        both = jnp.where(mask, landed, both_ref[here, :].astype(F32)).astype(BF16)
        keys_ref[here, :] = both[:, 0:HEAD]
        values_ref[here, :] = both[:, HEAD:]
    finish(fetch([(keys_ref, keys_out), (values_ref, values_out)], sems))


def merge(starts, arrived, both):
    shape = (both.shape[0], HEAD)
    return pl.pallas_call(
        merge_kernel,
        in_specs=[IN_VMEM, ANYWHERE, ANYWHERE],
        out_specs=[ANYWHERE] * 2,
        out_shape=[jax.ShapeDtypeStruct(shape, BF16)] * 2,
        scratch_shapes=[
            pltpu.VMEM(arrived.shape, BF16),
            pltpu.VMEM(both.shape, BF16),
            pltpu.VMEM(shape, BF16),
            pltpu.VMEM(shape, BF16),
            pltpu.SemaphoreType.DMA((2,)),
        ],
        compiler_params=PARAMS,
        cost_estimate=SMALL,
        name="merge",
    )(starts, arrived, both)


def hold_kernel(*refs):
    count = (len(refs) - 1) // 2
    copies = []
    for n, (source, target) in enumerate(zip(refs[0:count], refs[count : 2 * count])):
        half = source.shape[0] // 2
        spans = [pl.ds(0, half), pl.ds(half, half)]
        copies += fetch([(source.at[p], target.at[p]) for p in spans], refs[-1], 2 * n)
    finish(copies)


def hold(*arrays):
    return pl.pallas_call(
        hold_kernel,
        in_specs=[ANYWHERE] * len(arrays),
        out_specs=[IN_VMEM] * len(arrays),
        out_shape=[pltpu.VMEM(x.shape, x.dtype) for x in arrays],
        scratch_shapes=[pltpu.SemaphoreType.DMA((2 * len(arrays),))],
        compiler_params=PARAMS,
        cost_estimate=SMALL,
        name="hold",
    )(*[far(x) for x in arrays])


TILE = 256


def backward_kernel(first, masked, x_ref, gain_ref, starts_ref, squares_ref, wk_ref, wv_ref, *rest):
    resids, (out_ref, keys_all, values_all, held, sems) = rest[0:CHUNKS], rest[CHUNKS:]
    rows, width = x_ref.shape
    if masked:
        mask = image_rows_mask(rows, 0, first_rows(starts_ref, rows)[1])
    inverse = inverse_of(squares_ref[...], first, rows)
    lanes = no_lanes()
    for n, ref in enumerate(resids):
        here = head_columns((RINGS - n) % RINGS, n >= RINGS)
        keys_all[:, here] = ref[0:rows, 0:HEAD]
        values_all[:, here] = ref[0:rows, HEAD:]
        lanes = lanes + join_extra(ref[rows:, :])
    coefficient = inverse * inverse * lanes_to_column(lanes, 0, rows) / WIDTH
    contract = (((1,), (1,)), ((), ()))
    out = []
    for n in range(width // TILE):
        here = slice(n * TILE, (n + 1) * TILE)
        back = lax.dot_general(
            keys_all[...], wk_ref[here, :], contract, preferred_element_type=F32
        ) + lax.dot_general(values_all[...], wv_ref[here, :], contract, preferred_element_type=F32)
        grad = gain_ref[:, here] * inverse * back - coefficient * x_ref[:, here].astype(F32)
        if masked:
            grad = jnp.where(mask, 0.0, grad)
        held[:, here] = grad.astype(BF16)
        span = pl.ds(n * TILE, TILE)
        out += fetch([(held.at[:, span], out_ref.at[:, span])], sems, n)
    finish(out)


def backward(x, gain, squares, first, weights, starts, resids, masked):
    rows, width = x.shape
    columns = weights[0].shape[1]
    return pl.pallas_call(
        functools.partial(backward_kernel, first, masked),
        in_specs=[IN_VMEM] * (6 + CHUNKS),
        out_specs=ANYWHERE,
        out_shape=jax.ShapeDtypeStruct(x.shape, BF16),
        scratch_shapes=[
            pltpu.VMEM((rows, columns), BF16),
            pltpu.VMEM((rows, columns), BF16),
            pltpu.VMEM(x.shape, BF16),
            pltpu.SemaphoreType.DMA((width // TILE,)),
        ],
        compiler_params=PARAMS,
        cost_estimate=SMALL,
        name="backward",
    )(near(x), gain, starts, squares, *[near(w) for w in weights], *[near(r) for r in resids])


def around(x, shift):
    return lax.ppermute(
        x, "tp", [(2 * y + c, 2 * ((y + shift) % RINGS) + c) for y in range(RINGS) for c in range(2)]
    )


def across(x):
    return lax.ppermute(x, "tp", [(i, i ^ 1) for i in range(2 * RINGS)])


def across_in_turn(own, before):
    other = []
    for x in own:
        before = across(after(x, before))
        other.append(before)
    return other


def route(x):
    return lax.all_to_all(x, "rows", split_axis=0, concat_axis=0, tiled=True)


def on_device(
    text_embed,
    image_embed,
    image_start,
    norm_gain,
    key_weight,
    value_weight,
    key_target,
    value_target,
):
    seq_rows = text_embed.shape[0]
    gain = norm_gain[None, :]
    starts = image_start[None, :]
    weights = (key_weight, value_weight)
    targets = (key_target, value_target)

    images = image_embed.shape[0]
    early, late = (2,), (1, 3, 0)
    sent_early, sent_late, scaled, lanes, *held = forward_other(
        text_embed, image_embed, gain, weights, (early, late)
    )
    arrived_early = across(sent_early)
    arrived_late = across(after(sent_late, arrived_early))
    close = (2, 1, 3)
    sums = forward_own(scaled, lanes, held, arrived_early, early, close)
    sums |= forward_own(after(scaled, sums[2]), lanes, held, arrived_late, late, close)
    parts = [sums[0]] + [around(sums[d], d) for d in (2, 1, 3)]
    goals = route(gather_targets(after(starts, sums[0]), *targets))

    both, resid, squares = text_combine(parts, targets)
    resid1, resid2, resid3 = [around(resid, d) for d in (1, 2, 3)]
    parts[0] = after(parts[0], resid)
    image_send, image_both = image_keys(parts, starts, squares, images, seq_rows)
    image_resid = image_residual(image_both, goals, starts, seq_rows)
    landed = route(after(image_send, image_resid))
    image_resid2 = around(image_resid, 2)
    image_resid1 = around(after(image_resid, resid1), 1)
    image_resid3 = around(after(image_resid, resid3), 3)

    *held, text_held, image_held = hold(
        *weights, after(text_embed, resid1, resid2, resid3), after(image_embed, image_resid)
    )
    own = [resid, resid1, resid3, resid2]
    other = [across(r) for r in own]
    resids = [x[n] for x in (own, other) for n in (0, 1, 3, 2)]
    text_grad = backward(text_held, gain, squares, 0, held, starts, resids, True)
    own = [image_resid, image_resid1, image_resid3, image_resid2]
    own[1], own[2] = after(own[1], text_grad), after(own[2], text_grad)
    other = [across(r) for r in own]
    resids = [x[n] for x in (own, other) for n in (0, 1, 3, 2)]
    resids[0] = after(resids[0], text_grad)
    image_grad = backward(
        image_held, gain, squares, seq_rows // HEAD, held, starts, resids, False
    )
    keys, values = merge(after(starts, image_grad), landed, both)
    return (keys, values, text_grad, image_grad)


def solution(mesh):
    in_specs = (
        P("rows", "tp"),
        P("rows", "tp"),
        P(),
        P("tp"),
        P("tp", None),
        P("tp", None),
        P("rows", "tp"),
        P("rows", "tp"),
    )
    out_specs = (P("rows", "tp"), P("rows", "tp"), P("rows", "tp"), P("rows", "tp"))
    return jax.shard_map(
        on_device, mesh=mesh, in_specs=in_specs, out_specs=out_specs, check_vma=False
    )
```

```python
import functools

import jax
import jax.numpy as jnp
from jax import lax
from jax.experimental import pallas as pl
from jax.experimental.pallas import tpu as pltpu
from jax.sharding import PartitionSpec as P

WIDTH = 8192
EPSILON = 1e-06
IMAGE_LEN = 24
EXTRA = 16
HEAD = 128
PAIR = 2 * HEAD
RINGS = 4
CHUNKS = 2 * RINGS
PIECE = 128
ABSENT = 8192.0

F32 = jnp.float32
BF16 = jnp.bfloat16
PARAMS = pltpu.CompilerParams(vmem_limit_bytes=24 * 2**20)
IN_VMEM = pl.BlockSpec(memory_space=pltpu.VMEM)
ANYWHERE = pl.BlockSpec(memory_space=pl.ANY)


def near(x):
    return pltpu.with_memory_space_constraint(x, pltpu.VMEM)


def far(x):
    return pltpu.with_memory_space_constraint(x, pltpu.HBM)


def after(x, *others):
    return lax.optimization_barrier((x, *others))[0]


def fetch(pairs, sems, first=0):
    copies = [
        pltpu.make_async_copy(source, target, sems.at[first + n])
        for n, (source, target) in enumerate(pairs)
    ]
    for copy in copies:
        copy.start()
    return copies


def finish(copies):
    for copy in copies:
        copy.wait()


SMALL = pl.CostEstimate(flops=2**20, bytes_accessed=2**16, transcendentals=0)


def same_index(count):
    shape = (count, count)
    return lax.broadcasted_iota(jnp.int32, shape, 0) == lax.broadcasted_iota(jnp.int32, shape, 1)


def with_piece(lanes, p, column):
    line = jnp.sum(jnp.where(same_index(HEAD), column, 0.0), axis=0, keepdims=True)
    return jnp.where(lax.broadcasted_iota(jnp.int32, lanes.shape, 0) == p, line, lanes)


def with_column(lanes, column, first=0):
    for p in range(column.shape[0] // HEAD):
        lanes = with_piece(lanes, first + p, column[p * HEAD : (p + 1) * HEAD, :])
    return lanes


def lanes_to_column(lanes, first, rows):
    eye = same_index(HEAD)
    pieces = [
        jnp.sum(jnp.where(eye, lanes[p : p + 1, :], 0.0), axis=1, keepdims=True)
        for p in range(first, first + rows // HEAD)
    ]
    return jnp.concatenate(pieces, axis=0)


def no_lanes():
    return jnp.zeros((EXTRA, HEAD), F32)


def split_extra(lanes):
    high = lanes.astype(BF16).astype(F32)
    return jnp.concatenate([high, lanes - high], axis=1).astype(BF16)


def join_extra(block):
    block = block.astype(F32)
    return block[:, 0:HEAD] + block[:, HEAD:]


def my_place():
    mine = lax.axis_index("tp")
    return lax.div(mine, 2), lax.rem(mine, 2)


def head_columns(d, other):
    ring, core = my_place()
    chip = lax.rem(ring + d, RINGS)
    return pl.ds(pl.multiple_of(HEAD * (2 * chip + (1 - core if other else core)), HEAD), HEAD)


def pair_weight(wk_ref, wv_ref, d, other):
    here = head_columns(d, other)
    return jnp.concatenate([wk_ref[:, here], wv_ref[:, here]], axis=1)


def forward_other_kernel(
    splits, text_ref, image_ref, gain_ref, wk_from, wv_from,
    early_ref, late_ref, scaled_ref, lanes_ref, wk_ref, wv_ref, held, sems, more,
):
    rows, depth = scaled_ref.shape
    pairs = []
    for ref in (text_ref, image_ref):
        for p in range(ref.shape[0] // PIECE):
            to = held.at[pl.ds(len(pairs) * PIECE, PIECE)]
            pairs.append((ref.at[pl.ds(p * PIECE, PIECE)], to))
    x_copies = fetch(pairs, sems)
    spans = [pl.ds(p * PAIR, PAIR) for p in range(depth // PAIR)]
    weights = [(wk_from.at[p], wk_ref.at[p]) for p in spans]
    weights += [(wv_from.at[p], wv_ref.at[p]) for p in spans]
    weights = fetch(weights, more)
    lanes = no_lanes()
    for p, copy in enumerate(x_copies):
        copy.wait()
        here = slice(p * PIECE, (p + 1) * PIECE)
        x = held[here, :].astype(F32)
        scaled_ref[here, :] = (gain_ref[...] * x).astype(BF16)
        lanes = with_piece(lanes, p, jnp.sum(x * x, axis=1, keepdims=True))
    lanes_ref[...] = lanes
    extra = split_extra(lanes)
    finish(weights)
    for split, send_ref in zip(splits, (early_ref, late_ref)):
        for n, d in enumerate(split):
            weight = pair_weight(wk_ref, wv_ref, d, True)
            product = jnp.dot(scaled_ref[...], weight, preferred_element_type=F32)
            send_ref[n, 0:rows, :] = product.astype(BF16)
            send_ref[n, rows:, :] = extra


def forward_other(text, image, gain, weights, splits):
    rows, width = text.shape[0] + image.shape[0], text.shape[1]
    out_shape = [pltpu.VMEM((len(split), rows + EXTRA, PAIR), BF16) for split in splits] + [
        pltpu.VMEM((rows, width), BF16),
        pltpu.VMEM((EXTRA, HEAD), F32),
    ]
    out_shape += [pltpu.VMEM(w.shape, BF16) for w in weights]
    return pl.pallas_call(
        functools.partial(forward_other_kernel, splits),
        in_specs=[ANYWHERE, ANYWHERE, IN_VMEM, ANYWHERE, ANYWHERE],
        out_specs=[IN_VMEM] * len(out_shape),
        out_shape=out_shape,
        scratch_shapes=[
            pltpu.VMEM((rows, width), BF16),
            pltpu.SemaphoreType.DMA((rows // PIECE,)),
            pltpu.SemaphoreType.DMA((2 * width // PAIR,)),
        ],
        compiler_params=PARAMS,
        cost_estimate=SMALL,
        name="forward_other",
    )(far(text), far(image), gain, *[far(w) for w in weights])


def forward_own_kernel(split, close, scaled_ref, lanes_ref, wk_ref, wv_ref, in_ref, *refs):
    out_refs, (held, sems) = refs[0 : len(split)], refs[len(split) :]
    rows = scaled_ref.shape[0]
    extra = split_extra(lanes_ref[...] + join_extra(in_ref[0, rows:, :]))
    copies = []
    for n, d in enumerate(split):
        weight = pair_weight(wk_ref, wv_ref, d, False)
        product = jnp.dot(scaled_ref[...], weight, preferred_element_type=F32)
        total = (product + in_ref[n, 0:rows, :].astype(F32)).astype(BF16)
        if d in close:
            out_refs[n][0:rows, :] = total
            out_refs[n][rows:, :] = extra
        else:
            held[n, 0:rows, :] = total
            held[n, rows:, :] = extra
            copies += fetch([(held.at[n], out_refs[n])], sems, n)
    finish(copies)


def forward_own(scaled, lanes, weights, arrived, split, close):
    rows, width = scaled.shape
    block = (rows + EXTRA, PAIR)
    sums = pl.pallas_call(
        functools.partial(forward_own_kernel, split, close),
        in_specs=[IN_VMEM] * 5,
        out_specs=[IN_VMEM if d in close else ANYWHERE for d in split],
        out_shape=[(pltpu.VMEM if d in close else pltpu.HBM)(block, BF16) for d in split],
        scratch_shapes=[
            pltpu.VMEM((len(split),) + block, BF16),
            pltpu.SemaphoreType.DMA((len(split),)),
        ],
        compiler_params=PARAMS,
        cost_estimate=SMALL,
        name="forward_own",
    )(near(scaled), near(lanes), *[near(w) for w in weights], near(arrived))
    return dict(zip(split, sums))


def inverse_of(squares, first, rows):
    return lax.rsqrt(lanes_to_column(squares, first, rows) / WIDTH + EPSILON)


def total_of(parts):
    total = parts[0].astype(F32)
    for d in range(1, RINGS):
        total = total + parts[d].astype(F32)
    return total


def residual(both, target):
    both = both.astype(F32)
    resid = (both - target.astype(F32)).astype(BF16)
    return resid, jnp.sum(resid.astype(F32) * both, axis=1, keepdims=True)


def text_combine_kernel(
    a, b, c, d, kt_ref, vt_ref, both_out, resid_out, squares_ref,
    parts, extras, targets, both_ref, resid_ref, sems, more, stores,
):
    rows, all_rows = both_ref.shape[0], a.shape[0] - EXTRA
    step = PAIR
    tail = pl.ds(all_rows, EXTRA)
    spare = fetch([(ref.at[tail], extras.at[n]) for n, ref in enumerate((a, b, c, d))], more)
    loads = []
    for begin in range(0, rows, step):
        span = pl.ds(begin, step)
        pairs = [(ref.at[span], parts.at[n, span]) for n, ref in enumerate((a, b, c, d))]
        pairs += [(ref.at[span], targets.at[n, span]) for n, ref in enumerate((kt_ref, vt_ref))]
        loads.append(fetch(pairs, sems, len(loads) * (RINGS + 2)))
    finish(spare)
    squares = total_of([join_extra(extras[n]) for n in range(RINGS)])
    squares_ref[...] = squares
    lanes, out = no_lanes(), []
    for n, begin in enumerate(range(0, rows, step)):
        here, span = slice(begin, begin + step), pl.ds(begin, step)
        inverse = inverse_of(squares, begin // HEAD, step)
        finish(loads[n])
        total = total_of([parts[m, here, :] for m in range(RINGS)])
        both = (inverse * total).astype(BF16)
        target = jnp.concatenate([targets[0, here, :], targets[1, here, :]], axis=1)
        resid, dots = residual(both, target)
        resid_ref[here, :] = resid
        both_ref[here, :] = both
        pairs = [(resid_ref.at[span], resid_out.at[span]), (both_ref.at[span], both_out.at[span])]
        out += fetch(pairs, stores, 2 * n)
        lanes = with_column(lanes, dots, begin // HEAD)
    resid_ref[rows:, :] = split_extra(lanes)
    tail = pl.ds(rows, EXTRA)
    out += fetch([(resid_ref.at[tail], resid_out.at[tail])], stores, len(out))
    finish(out)


def text_combine(parts, targets):
    rows = targets[0].shape[0]
    shapes = [((rows, PAIR), BF16), ((rows + EXTRA, PAIR), BF16)]
    steps = rows // PAIR
    return pl.pallas_call(
        text_combine_kernel,
        in_specs=[ANYWHERE] * 6,
        out_specs=[ANYWHERE] * 2 + [IN_VMEM],
        out_shape=[*[pltpu.HBM(*s) for s in shapes], jax.ShapeDtypeStruct((EXTRA, HEAD), F32)],
        scratch_shapes=[
            pltpu.VMEM((RINGS, rows, PAIR), BF16),
            pltpu.VMEM((RINGS, EXTRA, PAIR), BF16),
            pltpu.VMEM((2,) + targets[0].shape, BF16),
            *[pltpu.VMEM(*s) for s in shapes],
            pltpu.SemaphoreType.DMA((steps * (RINGS + 2),)),
            pltpu.SemaphoreType.DMA((RINGS,)),
            pltpu.SemaphoreType.DMA((2 * steps + 1,)),
        ],
        compiler_params=PARAMS,
        cost_estimate=SMALL,
        name="text_combine",
    )(far(parts[0]), *parts[1:], *[far(t) for t in targets])


def one_hot(match):
    return jnp.where(match, jnp.ones(match.shape, F32), jnp.zeros(match.shape, F32)).astype(BF16)


def slot_columns(rows, first, lanes):
    shape = (rows, lanes.shape[1])
    row = first + lax.broadcasted_iota(jnp.int32, shape, 0)
    begin = IMAGE_LEN * lax.broadcasted_iota(jnp.int32, shape, 1)
    inside = (row >= begin) & (row < begin + IMAGE_LEN)
    value = lanes + (row - begin).astype(F32)
    return jnp.sum(jnp.where(inside, value, 0.0), axis=1, keepdims=True)


def slot_lanes(rows, column):
    shape = (column.shape[0], rows)
    row = lax.broadcasted_iota(jnp.int32, shape, 1)
    begin = IMAGE_LEN * lax.broadcasted_iota(jnp.int32, shape, 0)
    inside = (row >= begin) & (row < begin + IMAGE_LEN)
    value = column + (row - begin).astype(F32)
    return jnp.sum(jnp.where(inside, value, 0.0), axis=0, keepdims=True)


def first_rows(starts_ref, rows):
    shards = lax.axis_size("rows")
    images = starts_ref.shape[1] // shards
    offset = starts_ref[...].astype(F32) - (lax.axis_index("rows") * rows).astype(F32)
    value = jnp.where((offset >= 0.0) & (offset < rows), offset + ABSENT, 0.0)
    shape = (shards, starts_ref.shape[1])
    lane = lax.broadcasted_iota(jnp.int32, shape, 1)
    begin = images * lax.broadcasted_iota(jnp.int32, shape, 0)
    mine = (lane >= begin) & (lane < begin + images)
    column = jnp.sum(jnp.where(mine, value, 0.0), axis=1, keepdims=True) - ABSENT
    return column, jnp.sum(jnp.where(same_index(shards), column, 0.0), axis=0, keepdims=True)


def destinations(starts_ref, rows):
    images = starts_ref.shape[1] // lax.axis_size("rows")
    slot = IMAGE_LEN * jnp.floor((starts_ref[...].astype(F32) + 0.5) / rows)
    shape = (images, starts_ref.shape[1])
    image = lax.axis_index("rows") * images + lax.broadcasted_iota(jnp.int32, shape, 0)
    mine = lax.broadcasted_iota(jnp.int32, shape, 1) == image
    column = jnp.sum(jnp.where(mine, slot, 0.0), axis=1, keepdims=True)
    return jnp.sum(jnp.where(same_index(images), column, 0.0), axis=0, keepdims=True), column


def image_keys_kernel(
    seq_rows, a, b, c, d, starts_ref, squares_ref, send_out, both_out,
    parts, send_ref, both_ref, sems,
):
    rows, slots = both_ref.shape[0], send_ref.shape[0]
    span = pl.ds(seq_rows, rows)
    copies = fetch([(ref.at[span], parts.at[n]) for n, ref in enumerate((a, b, c, d))], sems)
    _, dest = destinations(starts_ref, seq_rows)
    slot = lax.broadcasted_iota(jnp.int32, (slots, rows), 0).astype(F32)
    picks = one_hot(slot == slot_lanes(rows, dest))
    inverse = inverse_of(squares_ref[...], seq_rows // HEAD, rows)
    finish(copies)
    both = (inverse * total_of([parts[n] for n in range(RINGS)])).astype(BF16)
    both_ref[...] = both
    out = fetch([(both_ref, both_out)], sems)
    send_ref[...] = jnp.dot(picks, both, preferred_element_type=F32).astype(BF16)
    out += fetch([(send_ref, send_out)], sems, 1)
    finish(out)


def image_keys(parts, starts, squares, rows, seq_rows):
    slots = lax.axis_size("rows") * IMAGE_LEN
    shapes = [((slots, PAIR), BF16), ((rows, PAIR), BF16)]
    return pl.pallas_call(
        functools.partial(image_keys_kernel, seq_rows),
        in_specs=[ANYWHERE] * RINGS + [IN_VMEM] * 2,
        out_specs=[ANYWHERE] * 2,
        out_shape=[pltpu.HBM(*s) for s in shapes],
        scratch_shapes=[
            pltpu.VMEM((RINGS, rows, PAIR), BF16),
            *[pltpu.VMEM(*s) for s in shapes],
            pltpu.SemaphoreType.DMA((RINGS,)),
        ],
        compiler_params=PARAMS,
        cost_estimate=SMALL,
        name="image_keys",
    )(far(parts[0]), *parts[1:], starts, squares)


def image_residual_kernel(
    seq_rows, both_from, arrived_from, starts_ref, resid_out, both_ref, arrived_ref, resid_ref, sems
):
    copies = fetch([(both_from, both_ref), (arrived_from, arrived_ref)], sems)
    rows = both_ref.shape[0]
    dest, _ = destinations(starts_ref, seq_rows)
    shape = (rows, arrived_ref.shape[0])
    slot = lax.broadcasted_iota(jnp.int32, shape, 1).astype(F32)
    picks = one_hot(slot == slot_columns(rows, 0, dest))
    finish(copies)
    target = jnp.dot(picks, arrived_ref[...], preferred_element_type=F32)
    resid, dots = residual(both_ref[...], target)
    resid_ref[0:rows, :] = resid
    resid_ref[rows:, :] = split_extra(with_column(no_lanes(), dots))
    finish(fetch([(resid_ref, resid_out)], sems))


def image_residual(both, arrived, starts, seq_rows):
    shape = (both.shape[0] + EXTRA, PAIR)
    return pl.pallas_call(
        functools.partial(image_residual_kernel, seq_rows),
        in_specs=[ANYWHERE, ANYWHERE, IN_VMEM],
        out_specs=ANYWHERE,
        out_shape=pltpu.HBM(shape, BF16),
        scratch_shapes=[
            pltpu.VMEM(both.shape, BF16),
            pltpu.VMEM(arrived.shape, BF16),
            pltpu.VMEM(shape, BF16),
            pltpu.SemaphoreType.DMA((2,)),
        ],
        compiler_params=PARAMS,
        cost_estimate=SMALL,
        name="image_residual",
    )(far(both), arrived, starts)


def gather_kernel(starts_ref, kt_from, vt_from, out_ref, halves, target_ref, held, sems):
    copies = fetch([(kt_from, halves.at[0]), (vt_from, halves.at[1])], sems)
    rows = target_ref.shape[0]
    _, first = first_rows(starts_ref, rows)
    finish(copies)
    target_ref[:, 0:HEAD] = halves[0]
    target_ref[:, HEAD:] = halves[1]
    for begin in range(0, out_ref.shape[0], PAIR):
        place = slot_columns(PAIR, begin, first)
        position = lax.broadcasted_iota(jnp.int32, (PAIR, rows), 1).astype(F32)
        picked = jnp.dot(
            one_hot(position == place), target_ref[...], preferred_element_type=F32
        )
        held[begin : begin + PAIR, :] = picked.astype(BF16)
    finish(fetch([(held, out_ref)], sems))


def gather_targets(starts, key_target, value_target):
    shape = (lax.axis_size("rows") * IMAGE_LEN, PAIR)
    return pl.pallas_call(
        gather_kernel,
        in_specs=[IN_VMEM, ANYWHERE, ANYWHERE],
        out_specs=ANYWHERE,
        out_shape=pltpu.HBM(shape, BF16),
        scratch_shapes=[
            pltpu.VMEM((2,) + key_target.shape, BF16),
            pltpu.VMEM((key_target.shape[0], PAIR), BF16),
            pltpu.VMEM(shape, BF16),
            pltpu.SemaphoreType.DMA((2,)),
        ],
        compiler_params=PARAMS,
        cost_estimate=SMALL,
        name="gather_targets",
    )(starts, far(key_target), far(value_target))


def image_rows_mask(rows, first_row, first_lanes):
    shape = (rows, first_lanes.shape[1])
    row = (first_row + lax.broadcasted_iota(jnp.int32, shape, 0)).astype(F32)
    inside = (row >= first_lanes) & (row < first_lanes + IMAGE_LEN)
    return jnp.sum(jnp.where(inside, 1.0, 0.0), axis=1, keepdims=True) > 0.5


def merge_kernel(
    starts_ref, arrived_from, both_from, keys_out, values_out,
    arrived_ref, both_ref, keys_ref, values_ref, sems,
):
    copies = fetch([(arrived_from, arrived_ref), (both_from, both_ref)], sems)
    slots, rows = arrived_ref.shape[0], both_ref.shape[0]
    column, lanes = first_rows(starts_ref, rows)
    place = slot_lanes(slots, column)
    finish(copies)
    for begin in range(0, rows, PAIR):
        row = begin + lax.broadcasted_iota(jnp.int32, (PAIR, slots), 0)
        picks = one_hot(row.astype(F32) == place)
        landed = jnp.dot(picks, arrived_ref[...], preferred_element_type=F32)
        here = slice(begin, begin + PAIR)
        mask = image_rows_mask(PAIR, begin, lanes)
        both = jnp.where(mask, landed, both_ref[here, :].astype(F32)).astype(BF16)
        keys_ref[here, :] = both[:, 0:HEAD]
        values_ref[here, :] = both[:, HEAD:]
    finish(fetch([(keys_ref, keys_out), (values_ref, values_out)], sems))


def merge(starts, arrived, both):
    shape = (both.shape[0], HEAD)
    return pl.pallas_call(
        merge_kernel,
        in_specs=[IN_VMEM, ANYWHERE, ANYWHERE],
        out_specs=[ANYWHERE] * 2,
        out_shape=[jax.ShapeDtypeStruct(shape, BF16)] * 2,
        scratch_shapes=[
            pltpu.VMEM(arrived.shape, BF16),
            pltpu.VMEM(both.shape, BF16),
            pltpu.VMEM(shape, BF16),
            pltpu.VMEM(shape, BF16),
            pltpu.SemaphoreType.DMA((2,)),
        ],
        compiler_params=PARAMS,
        cost_estimate=SMALL,
        name="merge",
    )(starts, arrived, both)


def hold_kernel(*refs):
    count = (len(refs) - 1) // 2
    copies = []
    for n, (source, target) in enumerate(zip(refs[0:count], refs[count : 2 * count])):
        half = source.shape[0] // 2
        spans = [pl.ds(0, half), pl.ds(half, half)]
        copies += fetch([(source.at[p], target.at[p]) for p in spans], refs[-1], 2 * n)
    finish(copies)


def hold(*arrays):
    return pl.pallas_call(
        hold_kernel,
        in_specs=[ANYWHERE] * len(arrays),
        out_specs=[IN_VMEM] * len(arrays),
        out_shape=[pltpu.VMEM(x.shape, x.dtype) for x in arrays],
        scratch_shapes=[pltpu.SemaphoreType.DMA((2 * len(arrays),))],
        compiler_params=PARAMS,
        cost_estimate=SMALL,
        name="hold",
    )(*[far(x) for x in arrays])


TILE = 256


def backward_kernel(first, masked, x_ref, gain_ref, starts_ref, squares_ref, wk_ref, wv_ref, *rest):
    resids, (out_ref, keys_all, values_all, held, sems) = rest[0:CHUNKS], rest[CHUNKS:]
    rows, width = x_ref.shape
    if masked:
        mask = image_rows_mask(rows, 0, first_rows(starts_ref, rows)[1])
    inverse = inverse_of(squares_ref[...], first, rows)
    lanes = no_lanes()
    for n, ref in enumerate(resids):
        here = head_columns((RINGS - n) % RINGS, n >= RINGS)
        keys_all[:, here] = ref[0:rows, 0:HEAD]
        values_all[:, here] = ref[0:rows, HEAD:]
        lanes = lanes + join_extra(ref[rows:, :])
    coefficient = inverse * inverse * lanes_to_column(lanes, 0, rows) / WIDTH
    contract = (((1,), (1,)), ((), ()))
    out = []
    for n in range(width // TILE):
        here = slice(n * TILE, (n + 1) * TILE)
        back = lax.dot_general(
            keys_all[...], wk_ref[here, :], contract, preferred_element_type=F32
        ) + lax.dot_general(values_all[...], wv_ref[here, :], contract, preferred_element_type=F32)
        grad = gain_ref[:, here] * inverse * back - coefficient * x_ref[:, here].astype(F32)
        if masked:
            grad = jnp.where(mask, 0.0, grad)
        held[:, here] = grad.astype(BF16)
        span = pl.ds(n * TILE, TILE)
        out += fetch([(held.at[:, span], out_ref.at[:, span])], sems, n)
    finish(out)


def backward(x, gain, squares, first, weights, starts, resids, masked):
    rows, width = x.shape
    columns = weights[0].shape[1]
    return pl.pallas_call(
        functools.partial(backward_kernel, first, masked),
        in_specs=[IN_VMEM] * (6 + CHUNKS),
        out_specs=ANYWHERE,
        out_shape=jax.ShapeDtypeStruct(x.shape, BF16),
        scratch_shapes=[
            pltpu.VMEM((rows, columns), BF16),
            pltpu.VMEM((rows, columns), BF16),
            pltpu.VMEM(x.shape, BF16),
            pltpu.SemaphoreType.DMA((width // TILE,)),
        ],
        compiler_params=PARAMS,
        cost_estimate=SMALL,
        name="backward",
    )(near(x), gain, starts, squares, *[near(w) for w in weights], *[near(r) for r in resids])


def around(x, shift):
    return lax.ppermute(
        x, "tp", [(2 * y + c, 2 * ((y + shift) % RINGS) + c) for y in range(RINGS) for c in range(2)]
    )


def across(x):
    return lax.ppermute(x, "tp", [(i, i ^ 1) for i in range(2 * RINGS)])


def across_in_turn(own, before):
    other = []
    for x in own:
        before = across(after(x, before))
        other.append(before)
    return other


def route(x):
    return lax.all_to_all(x, "rows", split_axis=0, concat_axis=0, tiled=True)


def on_device(
    text_embed,
    image_embed,
    image_start,
    norm_gain,
    key_weight,
    value_weight,
    key_target,
    value_target,
):
    seq_rows = text_embed.shape[0]
    gain = norm_gain[None, :]
    starts = image_start[None, :]
    weights = (key_weight, value_weight)
    targets = (key_target, value_target)

    images = image_embed.shape[0]
    early, late = (2,), (1, 3, 0)
    sent_early, sent_late, scaled, lanes, *held = forward_other(
        text_embed, image_embed, gain, weights, (early, late)
    )
    arrived_early = across(sent_early)
    arrived_late = across(after(sent_late, arrived_early))
    close = (2, 1, 3)
    sums = forward_own(scaled, lanes, held, arrived_early, early, close)
    sums |= forward_own(after(scaled, sums[2]), lanes, held, arrived_late, late, close)
    parts = [sums[0]] + [around(sums[d], d) for d in (2, 1, 3)]
    goals = route(gather_targets(after(starts, sums[0]), *targets))

    both, resid, squares = text_combine(parts, targets)
    resid1, resid2, resid3 = [around(resid, d) for d in (1, 2, 3)]
    parts[0] = after(parts[0], resid)
    image_send, image_both = image_keys(parts, starts, squares, images, seq_rows)
    image_resid = image_residual(image_both, goals, starts, seq_rows)
    landed = route(after(image_send, image_resid))
    image_resid2 = around(image_resid, 2)
    image_resid1 = around(after(image_resid, resid1), 1)
    image_resid3 = around(after(image_resid, resid3), 3)

    *held, text_held, image_held = hold(
        *weights, after(text_embed, resid1, resid2, resid3), after(image_embed, image_resid)
    )
    own = [resid, resid1, resid3, resid2]
    other = [across(resid)] + [across(after(r, held[0])) for r in own[1:]]
    resids = [x[n] for x in (own, other) for n in (0, 1, 3, 2)]
    text_grad = backward(text_held, gain, squares, 0, held, starts, resids, True)
    own = [image_resid, image_resid1, image_resid3, image_resid2]
    own[1], own[2] = after(own[1], text_grad), after(own[2], text_grad)
    other = [across(r) for r in own]
    resids = [x[n] for x in (own, other) for n in (0, 1, 3, 2)]
    resids[0] = after(resids[0], text_grad)
    image_grad = backward(
        image_held, gain, squares, seq_rows // HEAD, held, starts, resids, False
    )
    keys, values = merge(after(starts, image_grad), landed, both)
    return (keys, values, text_grad, image_grad)


def solution(mesh):
    in_specs = (
        P("rows", "tp"),
        P("rows", "tp"),
        P(),
        P("tp"),
        P("tp", None),
        P("tp", None),
        P("rows", "tp"),
        P("rows", "tp"),
    )
    out_specs = (P("rows", "tp"), P("rows", "tp"), P("rows", "tp"), P("rows", "tp"))
    return jax.shard_map(
        on_device, mesh=mesh, in_specs=in_specs, out_specs=out_specs, check_vma=False
    )
```

```python
import functools

import jax
import jax.numpy as jnp
from jax import lax
from jax.experimental import pallas as pl
from jax.experimental.pallas import tpu as pltpu
from jax.sharding import PartitionSpec as P

WIDTH = 8192
EPSILON = 1e-06
IMAGE_LEN = 24
EXTRA = 16
HEAD = 128
PAIR = 2 * HEAD
RINGS = 4
CHUNKS = 2 * RINGS
PIECE = 128
ABSENT = 8192.0

F32 = jnp.float32
BF16 = jnp.bfloat16
PARAMS = pltpu.CompilerParams(vmem_limit_bytes=24 * 2**20)
IN_VMEM = pl.BlockSpec(memory_space=pltpu.VMEM)
ANYWHERE = pl.BlockSpec(memory_space=pl.ANY)


def near(x):
    return pltpu.with_memory_space_constraint(x, pltpu.VMEM)


def far(x):
    return pltpu.with_memory_space_constraint(x, pltpu.HBM)


def after(x, *others):
    return lax.optimization_barrier((x, *others))[0]


def fetch(pairs, sems, first=0):
    copies = [
        pltpu.make_async_copy(source, target, sems.at[first + n])
        for n, (source, target) in enumerate(pairs)
    ]
    for copy in copies:
        copy.start()
    return copies


def finish(copies):
    for copy in copies:
        copy.wait()


SMALL = pl.CostEstimate(flops=2**20, bytes_accessed=2**16, transcendentals=0)


def same_index(count):
    shape = (count, count)
    return lax.broadcasted_iota(jnp.int32, shape, 0) == lax.broadcasted_iota(jnp.int32, shape, 1)


def with_piece(lanes, p, column):
    line = jnp.sum(jnp.where(same_index(HEAD), column, 0.0), axis=0, keepdims=True)
    return jnp.where(lax.broadcasted_iota(jnp.int32, lanes.shape, 0) == p, line, lanes)


def with_column(lanes, column, first=0):
    for p in range(column.shape[0] // HEAD):
        lanes = with_piece(lanes, first + p, column[p * HEAD : (p + 1) * HEAD, :])
    return lanes


def lanes_to_column(lanes, first, rows):
    eye = same_index(HEAD)
    pieces = [
        jnp.sum(jnp.where(eye, lanes[p : p + 1, :], 0.0), axis=1, keepdims=True)
        for p in range(first, first + rows // HEAD)
    ]
    return jnp.concatenate(pieces, axis=0)


def no_lanes():
    return jnp.zeros((EXTRA, HEAD), F32)


def split_extra(lanes):
    high = lanes.astype(BF16).astype(F32)
    return jnp.concatenate([high, lanes - high], axis=1).astype(BF16)


def join_extra(block):
    block = block.astype(F32)
    return block[:, 0:HEAD] + block[:, HEAD:]


def my_place():
    mine = lax.axis_index("tp")
    return lax.div(mine, 2), lax.rem(mine, 2)


def head_columns(d, other):
    ring, core = my_place()
    chip = lax.rem(ring + d, RINGS)
    return pl.ds(pl.multiple_of(HEAD * (2 * chip + (1 - core if other else core)), HEAD), HEAD)


def pair_weight(wk_ref, wv_ref, d, other):
    here = head_columns(d, other)
    return jnp.concatenate([wk_ref[:, here], wv_ref[:, here]], axis=1)


def forward_other_kernel(
    splits, text_ref, image_ref, gain_ref, wk_from, wv_from,
    early_ref, late_ref, scaled_ref, lanes_ref, wk_ref, wv_ref, held, sems, more,
):
    rows, depth = scaled_ref.shape
    pairs = []
    for ref in (text_ref, image_ref):
        for p in range(ref.shape[0] // PIECE):
            to = held.at[pl.ds(len(pairs) * PIECE, PIECE)]
            pairs.append((ref.at[pl.ds(p * PIECE, PIECE)], to))
    x_copies = fetch(pairs, sems)
    spans = [pl.ds(p * PAIR, PAIR) for p in range(depth // PAIR)]
    weights = [(wk_from.at[p], wk_ref.at[p]) for p in spans]
    weights += [(wv_from.at[p], wv_ref.at[p]) for p in spans]
    weights = fetch(weights, more)
    lanes = no_lanes()
    for p, copy in enumerate(x_copies):
        copy.wait()
        here = slice(p * PIECE, (p + 1) * PIECE)
        x = held[here, :].astype(F32)
        scaled_ref[here, :] = (gain_ref[...] * x).astype(BF16)
        lanes = with_piece(lanes, p, jnp.sum(x * x, axis=1, keepdims=True))
    lanes_ref[...] = lanes
    extra = split_extra(lanes)
    finish(weights)
    for split, send_ref in zip(splits, (early_ref, late_ref)):
        for n, d in enumerate(split):
            weight = pair_weight(wk_ref, wv_ref, d, True)
            product = jnp.dot(scaled_ref[...], weight, preferred_element_type=F32)
            send_ref[n, 0:rows, :] = product.astype(BF16)
            send_ref[n, rows:, :] = extra


def forward_other(text, image, gain, weights, splits):
    rows, width = text.shape[0] + image.shape[0], text.shape[1]
    out_shape = [pltpu.VMEM((len(split), rows + EXTRA, PAIR), BF16) for split in splits] + [
        pltpu.VMEM((rows, width), BF16),
        pltpu.VMEM((EXTRA, HEAD), F32),
    ]
    out_shape += [pltpu.VMEM(w.shape, BF16) for w in weights]
    return pl.pallas_call(
        functools.partial(forward_other_kernel, splits),
        in_specs=[ANYWHERE, ANYWHERE, IN_VMEM, ANYWHERE, ANYWHERE],
        out_specs=[IN_VMEM] * len(out_shape),
        out_shape=out_shape,
        scratch_shapes=[
            pltpu.VMEM((rows, width), BF16),
            pltpu.SemaphoreType.DMA((rows // PIECE,)),
            pltpu.SemaphoreType.DMA((2 * width // PAIR,)),
        ],
        compiler_params=PARAMS,
        cost_estimate=SMALL,
        name="forward_other",
    )(far(text), far(image), gain, *[far(w) for w in weights])


def forward_own_kernel(split, close, scaled_ref, lanes_ref, wk_ref, wv_ref, in_ref, *refs):
    out_refs, (held, sems) = refs[0 : len(split)], refs[len(split) :]
    rows = scaled_ref.shape[0]
    extra = split_extra(lanes_ref[...] + join_extra(in_ref[0, rows:, :]))
    copies = []
    for n, d in enumerate(split):
        weight = pair_weight(wk_ref, wv_ref, d, False)
        product = jnp.dot(scaled_ref[...], weight, preferred_element_type=F32)
        total = (product + in_ref[n, 0:rows, :].astype(F32)).astype(BF16)
        if d in close:
            out_refs[n][0:rows, :] = total
            out_refs[n][rows:, :] = extra
        else:
            held[n, 0:rows, :] = total
            held[n, rows:, :] = extra
            copies += fetch([(held.at[n], out_refs[n])], sems, n)
    finish(copies)


def forward_own(scaled, lanes, weights, arrived, split, close):
    rows, width = scaled.shape
    block = (rows + EXTRA, PAIR)
    sums = pl.pallas_call(
        functools.partial(forward_own_kernel, split, close),
        in_specs=[IN_VMEM] * 5,
        out_specs=[IN_VMEM if d in close else ANYWHERE for d in split],
        out_shape=[(pltpu.VMEM if d in close else pltpu.HBM)(block, BF16) for d in split],
        scratch_shapes=[
            pltpu.VMEM((len(split),) + block, BF16),
            pltpu.SemaphoreType.DMA((len(split),)),
        ],
        compiler_params=PARAMS,
        cost_estimate=SMALL,
        name="forward_own",
    )(near(scaled), near(lanes), *[near(w) for w in weights], near(arrived))
    return dict(zip(split, sums))


def inverse_of(squares, first, rows):
    return lax.rsqrt(lanes_to_column(squares, first, rows) / WIDTH + EPSILON)


def total_of(parts):
    total = parts[0].astype(F32)
    for d in range(1, RINGS):
        total = total + parts[d].astype(F32)
    return total


def residual(both, target):
    both = both.astype(F32)
    resid = (both - target.astype(F32)).astype(BF16)
    return resid, jnp.sum(resid.astype(F32) * both, axis=1, keepdims=True)


def text_combine_kernel(
    a, b, c, d, kt_ref, vt_ref, both_out, resid_out, squares_ref,
    parts, extras, targets, both_ref, resid_ref, sems, more, stores,
):
    rows, all_rows = both_ref.shape[0], a.shape[0] - EXTRA
    step = PAIR
    tail = pl.ds(all_rows, EXTRA)
    spare = fetch([(ref.at[tail], extras.at[n]) for n, ref in enumerate((a, b, c, d))], more)
    loads = []
    for begin in range(0, rows, step):
        span = pl.ds(begin, step)
        pairs = [(ref.at[span], parts.at[n, span]) for n, ref in enumerate((a, b, c, d))]
        pairs += [(ref.at[span], targets.at[n, span]) for n, ref in enumerate((kt_ref, vt_ref))]
        loads.append(fetch(pairs, sems, len(loads) * (RINGS + 2)))
    finish(spare)
    squares = total_of([join_extra(extras[n]) for n in range(RINGS)])
    squares_ref[...] = squares
    lanes, out = no_lanes(), []
    for n, begin in enumerate(range(0, rows, step)):
        here, span = slice(begin, begin + step), pl.ds(begin, step)
        inverse = inverse_of(squares, begin // HEAD, step)
        finish(loads[n])
        total = total_of([parts[m, here, :] for m in range(RINGS)])
        both = (inverse * total).astype(BF16)
        target = jnp.concatenate([targets[0, here, :], targets[1, here, :]], axis=1)
        resid, dots = residual(both, target)
        resid_ref[here, :] = resid
        both_ref[here, :] = both
        pairs = [(resid_ref.at[span], resid_out.at[span]), (both_ref.at[span], both_out.at[span])]
        out += fetch(pairs, stores, 2 * n)
        lanes = with_column(lanes, dots, begin // HEAD)
    resid_ref[rows:, :] = split_extra(lanes)
    tail = pl.ds(rows, EXTRA)
    out += fetch([(resid_ref.at[tail], resid_out.at[tail])], stores, len(out))
    finish(out)


def text_combine(parts, targets):
    rows = targets[0].shape[0]
    shapes = [((rows, PAIR), BF16), ((rows + EXTRA, PAIR), BF16)]
    steps = rows // PAIR
    return pl.pallas_call(
        text_combine_kernel,
        in_specs=[ANYWHERE] * 6,
        out_specs=[ANYWHERE] * 2 + [IN_VMEM],
        out_shape=[*[pltpu.HBM(*s) for s in shapes], jax.ShapeDtypeStruct((EXTRA, HEAD), F32)],
        scratch_shapes=[
            pltpu.VMEM((RINGS, rows, PAIR), BF16),
            pltpu.VMEM((RINGS, EXTRA, PAIR), BF16),
            pltpu.VMEM((2,) + targets[0].shape, BF16),
            *[pltpu.VMEM(*s) for s in shapes],
            pltpu.SemaphoreType.DMA((steps * (RINGS + 2),)),
            pltpu.SemaphoreType.DMA((RINGS,)),
            pltpu.SemaphoreType.DMA((2 * steps + 1,)),
        ],
        compiler_params=PARAMS,
        cost_estimate=SMALL,
        name="text_combine",
    )(far(parts[0]), *parts[1:], *[far(t) for t in targets])


def one_hot(match):
    return jnp.where(match, jnp.ones(match.shape, F32), jnp.zeros(match.shape, F32)).astype(BF16)


def slot_columns(rows, first, lanes):
    shape = (rows, lanes.shape[1])
    row = first + lax.broadcasted_iota(jnp.int32, shape, 0)
    begin = IMAGE_LEN * lax.broadcasted_iota(jnp.int32, shape, 1)
    inside = (row >= begin) & (row < begin + IMAGE_LEN)
    value = lanes + (row - begin).astype(F32)
    return jnp.sum(jnp.where(inside, value, 0.0), axis=1, keepdims=True)


def slot_lanes(rows, column):
    shape = (column.shape[0], rows)
    row = lax.broadcasted_iota(jnp.int32, shape, 1)
    begin = IMAGE_LEN * lax.broadcasted_iota(jnp.int32, shape, 0)
    inside = (row >= begin) & (row < begin + IMAGE_LEN)
    value = column + (row - begin).astype(F32)
    return jnp.sum(jnp.where(inside, value, 0.0), axis=0, keepdims=True)


def first_rows(starts_ref, rows):
    shards = lax.axis_size("rows")
    images = starts_ref.shape[1] // shards
    offset = starts_ref[...].astype(F32) - (lax.axis_index("rows") * rows).astype(F32)
    value = jnp.where((offset >= 0.0) & (offset < rows), offset + ABSENT, 0.0)
    shape = (shards, starts_ref.shape[1])
    lane = lax.broadcasted_iota(jnp.int32, shape, 1)
    begin = images * lax.broadcasted_iota(jnp.int32, shape, 0)
    mine = (lane >= begin) & (lane < begin + images)
    column = jnp.sum(jnp.where(mine, value, 0.0), axis=1, keepdims=True) - ABSENT
    return column, jnp.sum(jnp.where(same_index(shards), column, 0.0), axis=0, keepdims=True)


def destinations(starts_ref, rows):
    images = starts_ref.shape[1] // lax.axis_size("rows")
    slot = IMAGE_LEN * jnp.floor((starts_ref[...].astype(F32) + 0.5) / rows)
    shape = (images, starts_ref.shape[1])
    image = lax.axis_index("rows") * images + lax.broadcasted_iota(jnp.int32, shape, 0)
    mine = lax.broadcasted_iota(jnp.int32, shape, 1) == image
    column = jnp.sum(jnp.where(mine, slot, 0.0), axis=1, keepdims=True)
    return jnp.sum(jnp.where(same_index(images), column, 0.0), axis=0, keepdims=True), column


def image_keys_kernel(
    seq_rows, a, b, c, d, starts_ref, squares_ref, send_out, both_out,
    parts, send_ref, both_ref, sems,
):
    rows, slots = both_ref.shape[0], send_ref.shape[0]
    span = pl.ds(seq_rows, rows)
    copies = fetch([(ref.at[span], parts.at[n]) for n, ref in enumerate((a, b, c, d))], sems)
    _, dest = destinations(starts_ref, seq_rows)
    slot = lax.broadcasted_iota(jnp.int32, (slots, rows), 0).astype(F32)
    picks = one_hot(slot == slot_lanes(rows, dest))
    inverse = inverse_of(squares_ref[...], seq_rows // HEAD, rows)
    finish(copies)
    both = (inverse * total_of([parts[n] for n in range(RINGS)])).astype(BF16)
    both_ref[...] = both
    out = fetch([(both_ref, both_out)], sems)
    send_ref[...] = jnp.dot(picks, both, preferred_element_type=F32).astype(BF16)
    out += fetch([(send_ref, send_out)], sems, 1)
    finish(out)


def image_keys(parts, starts, squares, rows, seq_rows):
    slots = lax.axis_size("rows") * IMAGE_LEN
    shapes = [((slots, PAIR), BF16), ((rows, PAIR), BF16)]
    return pl.pallas_call(
        functools.partial(image_keys_kernel, seq_rows),
        in_specs=[ANYWHERE] * RINGS + [IN_VMEM] * 2,
        out_specs=[ANYWHERE] * 2,
        out_shape=[pltpu.HBM(*s) for s in shapes],
        scratch_shapes=[
            pltpu.VMEM((RINGS, rows, PAIR), BF16),
            *[pltpu.VMEM(*s) for s in shapes],
            pltpu.SemaphoreType.DMA((RINGS,)),
        ],
        compiler_params=PARAMS,
        cost_estimate=SMALL,
        name="image_keys",
    )(far(parts[0]), *parts[1:], starts, squares)


def image_residual_kernel(
    seq_rows, both_from, arrived_from, starts_ref, resid_out, both_ref, arrived_ref, resid_ref, sems
):
    copies = fetch([(both_from, both_ref), (arrived_from, arrived_ref)], sems)
    rows = both_ref.shape[0]
    dest, _ = destinations(starts_ref, seq_rows)
    shape = (rows, arrived_ref.shape[0])
    slot = lax.broadcasted_iota(jnp.int32, shape, 1).astype(F32)
    picks = one_hot(slot == slot_columns(rows, 0, dest))
    finish(copies)
    target = jnp.dot(picks, arrived_ref[...], preferred_element_type=F32)
    resid, dots = residual(both_ref[...], target)
    resid_ref[0:rows, :] = resid
    resid_ref[rows:, :] = split_extra(with_column(no_lanes(), dots))
    finish(fetch([(resid_ref, resid_out)], sems))


def image_residual(both, arrived, starts, seq_rows):
    shape = (both.shape[0] + EXTRA, PAIR)
    return pl.pallas_call(
        functools.partial(image_residual_kernel, seq_rows),
        in_specs=[ANYWHERE, ANYWHERE, IN_VMEM],
        out_specs=ANYWHERE,
        out_shape=pltpu.HBM(shape, BF16),
        scratch_shapes=[
            pltpu.VMEM(both.shape, BF16),
            pltpu.VMEM(arrived.shape, BF16),
            pltpu.VMEM(shape, BF16),
            pltpu.SemaphoreType.DMA((2,)),
        ],
        compiler_params=PARAMS,
        cost_estimate=SMALL,
        name="image_residual",
    )(far(both), arrived, starts)


def gather_kernel(starts_ref, kt_from, vt_from, out_ref, halves, target_ref, held, sems):
    copies = fetch([(kt_from, halves.at[0]), (vt_from, halves.at[1])], sems)
    rows = target_ref.shape[0]
    _, first = first_rows(starts_ref, rows)
    finish(copies)
    target_ref[:, 0:HEAD] = halves[0]
    target_ref[:, HEAD:] = halves[1]
    for begin in range(0, out_ref.shape[0], PAIR):
        place = slot_columns(PAIR, begin, first)
        position = lax.broadcasted_iota(jnp.int32, (PAIR, rows), 1).astype(F32)
        picked = jnp.dot(
            one_hot(position == place), target_ref[...], preferred_element_type=F32
        )
        held[begin : begin + PAIR, :] = picked.astype(BF16)
    finish(fetch([(held, out_ref)], sems))


def gather_targets(starts, key_target, value_target):
    shape = (lax.axis_size("rows") * IMAGE_LEN, PAIR)
    return pl.pallas_call(
        gather_kernel,
        in_specs=[IN_VMEM, ANYWHERE, ANYWHERE],
        out_specs=ANYWHERE,
        out_shape=pltpu.HBM(shape, BF16),
        scratch_shapes=[
            pltpu.VMEM((2,) + key_target.shape, BF16),
            pltpu.VMEM((key_target.shape[0], PAIR), BF16),
            pltpu.VMEM(shape, BF16),
            pltpu.SemaphoreType.DMA((2,)),
        ],
        compiler_params=PARAMS,
        cost_estimate=SMALL,
        name="gather_targets",
    )(starts, far(key_target), far(value_target))


def image_rows_mask(rows, first_row, first_lanes):
    shape = (rows, first_lanes.shape[1])
    row = (first_row + lax.broadcasted_iota(jnp.int32, shape, 0)).astype(F32)
    inside = (row >= first_lanes) & (row < first_lanes + IMAGE_LEN)
    return jnp.sum(jnp.where(inside, 1.0, 0.0), axis=1, keepdims=True) > 0.5


def merge_kernel(
    starts_ref, arrived_from, both_from, keys_out, values_out,
    arrived_ref, both_ref, keys_ref, values_ref, sems,
):
    copies = fetch([(arrived_from, arrived_ref), (both_from, both_ref)], sems)
    slots, rows = arrived_ref.shape[0], both_ref.shape[0]
    column, lanes = first_rows(starts_ref, rows)
    place = slot_lanes(slots, column)
    finish(copies)
    for begin in range(0, rows, PAIR):
        row = begin + lax.broadcasted_iota(jnp.int32, (PAIR, slots), 0)
        picks = one_hot(row.astype(F32) == place)
        landed = jnp.dot(picks, arrived_ref[...], preferred_element_type=F32)
        here = slice(begin, begin + PAIR)
        mask = image_rows_mask(PAIR, begin, lanes)
        both = jnp.where(mask, landed, both_ref[here, :].astype(F32)).astype(BF16)
        keys_ref[here, :] = both[:, 0:HEAD]
        values_ref[here, :] = both[:, HEAD:]
    finish(fetch([(keys_ref, keys_out), (values_ref, values_out)], sems))


def merge(starts, arrived, both):
    shape = (both.shape[0], HEAD)
    return pl.pallas_call(
        merge_kernel,
        in_specs=[IN_VMEM, ANYWHERE, ANYWHERE],
        out_specs=[ANYWHERE] * 2,
        out_shape=[jax.ShapeDtypeStruct(shape, BF16)] * 2,
        scratch_shapes=[
            pltpu.VMEM(arrived.shape, BF16),
            pltpu.VMEM(both.shape, BF16),
            pltpu.VMEM(shape, BF16),
            pltpu.VMEM(shape, BF16),
            pltpu.SemaphoreType.DMA((2,)),
        ],
        compiler_params=PARAMS,
        cost_estimate=SMALL,
        name="merge",
    )(starts, arrived, both)


def hold_kernel(*refs):
    count = (len(refs) - 1) // 2
    copies = []
    for n, (source, target) in enumerate(zip(refs[0:count], refs[count : 2 * count])):
        step = source.shape[0] // 4
        spans = [pl.ds(m * step, step) for m in range(4)]
        copies += fetch([(source.at[p], target.at[p]) for p in spans], refs[-1], 4 * n)
    finish(copies)


def hold(*arrays):
    return pl.pallas_call(
        hold_kernel,
        in_specs=[ANYWHERE] * len(arrays),
        out_specs=[IN_VMEM] * len(arrays),
        out_shape=[pltpu.VMEM(x.shape, x.dtype) for x in arrays],
        scratch_shapes=[pltpu.SemaphoreType.DMA((4 * len(arrays),))],
        compiler_params=PARAMS,
        cost_estimate=SMALL,
        name="hold",
    )(*[far(x) for x in arrays])


TILE = 256


def backward_kernel(first, masked, x_ref, gain_ref, starts_ref, squares_ref, wk_ref, wv_ref, *rest):
    resids, (out_ref, keys_all, values_all, held, sems) = rest[0:CHUNKS], rest[CHUNKS:]
    rows, width = x_ref.shape
    if masked:
        mask = image_rows_mask(rows, 0, first_rows(starts_ref, rows)[1])
    inverse = inverse_of(squares_ref[...], first, rows)
    lanes = no_lanes()
    for n, ref in enumerate(resids):
        here = head_columns((RINGS - n) % RINGS, n >= RINGS)
        keys_all[:, here] = ref[0:rows, 0:HEAD]
        values_all[:, here] = ref[0:rows, HEAD:]
        lanes = lanes + join_extra(ref[rows:, :])
    coefficient = inverse * inverse * lanes_to_column(lanes, 0, rows) / WIDTH
    contract = (((1,), (1,)), ((), ()))
    out = []
    for n in range(width // TILE):
        here = slice(n * TILE, (n + 1) * TILE)
        back = lax.dot_general(
            keys_all[...], wk_ref[here, :], contract, preferred_element_type=F32
        ) + lax.dot_general(values_all[...], wv_ref[here, :], contract, preferred_element_type=F32)
        grad = gain_ref[:, here] * inverse * back - coefficient * x_ref[:, here].astype(F32)
        if masked:
            grad = jnp.where(mask, 0.0, grad)
        held[:, here] = grad.astype(BF16)
        span = pl.ds(n * TILE, TILE)
        out += fetch([(held.at[:, span], out_ref.at[:, span])], sems, n)
    finish(out)


def backward(x, gain, squares, first, weights, starts, resids, masked):
    rows, width = x.shape
    columns = weights[0].shape[1]
    return pl.pallas_call(
        functools.partial(backward_kernel, first, masked),
        in_specs=[IN_VMEM] * (6 + CHUNKS),
        out_specs=ANYWHERE,
        out_shape=jax.ShapeDtypeStruct(x.shape, BF16),
        scratch_shapes=[
            pltpu.VMEM((rows, columns), BF16),
            pltpu.VMEM((rows, columns), BF16),
            pltpu.VMEM(x.shape, BF16),
            pltpu.SemaphoreType.DMA((width // TILE,)),
        ],
        compiler_params=PARAMS,
        cost_estimate=SMALL,
        name="backward",
    )(near(x), gain, starts, squares, *[near(w) for w in weights], *[near(r) for r in resids])


def around(x, shift):
    return lax.ppermute(
        x, "tp", [(2 * y + c, 2 * ((y + shift) % RINGS) + c) for y in range(RINGS) for c in range(2)]
    )


def across(x):
    return lax.ppermute(x, "tp", [(i, i ^ 1) for i in range(2 * RINGS)])


def across_in_turn(own, before):
    other = []
    for x in own:
        before = across(after(x, before))
        other.append(before)
    return other


def route(x):
    return lax.all_to_all(x, "rows", split_axis=0, concat_axis=0, tiled=True)


def on_device(
    text_embed,
    image_embed,
    image_start,
    norm_gain,
    key_weight,
    value_weight,
    key_target,
    value_target,
):
    seq_rows = text_embed.shape[0]
    gain = norm_gain[None, :]
    starts = image_start[None, :]
    weights = (key_weight, value_weight)
    targets = (key_target, value_target)

    images = image_embed.shape[0]
    early, late = (2,), (0, 1, 3)
    sent_early, sent_late, scaled, lanes, *held = forward_other(
        text_embed, image_embed, gain, weights, (early, late)
    )
    arrived_early = across(sent_early)
    arrived_late = across(after(sent_late, arrived_early))
    close = (2, 1, 3)
    sums = forward_own(scaled, lanes, held, arrived_early, early, close)
    sums |= forward_own(after(scaled, sums[2]), lanes, held, arrived_late, late, close)
    parts = [sums[0]] + [around(sums[d], d) for d in (2, 1, 3)]
    goals = route(gather_targets(after(starts, sums[0]), *targets))

    both, resid, squares = text_combine(parts, targets)
    resid1, resid2, resid3 = [around(resid, d) for d in (1, 2, 3)]
    parts[0] = after(parts[0], resid)
    image_send, image_both = image_keys(parts, starts, squares, images, seq_rows)
    image_resid = image_residual(image_both, goals, starts, seq_rows)
    landed = route(after(image_send, image_resid))
    image_resid2 = around(image_resid, 2)
    image_resid1 = around(after(image_resid, resid1), 1)
    image_resid3 = around(after(image_resid, resid3), 3)

    *held, text_held, image_held = hold(
        *weights, after(text_embed, resid1, resid2, resid3), after(image_embed, image_resid)
    )
    own = [resid, resid1, resid3, resid2]
    other = [across(resid)] + [across(after(r, held[0])) for r in own[1:]]
    resids = [x[n] for x in (own, other) for n in (0, 1, 3, 2)]
    text_grad = backward(text_held, gain, squares, 0, held, starts, resids, True)
    own = [image_resid, image_resid1, image_resid3, image_resid2]
    own[1], own[2] = after(own[1], text_grad), after(own[2], text_grad)
    other = [across(r) for r in own]
    resids = [x[n] for x in (own, other) for n in (0, 1, 3, 2)]
    resids[0] = after(resids[0], text_grad)
    image_grad = backward(
        image_held, gain, squares, seq_rows // HEAD, held, starts, resids, False
    )
    keys, values = merge(after(starts, image_grad), landed, both)
    return (keys, values, text_grad, image_grad)


def solution(mesh):
    in_specs = (
        P("rows", "tp"),
        P("rows", "tp"),
        P(),
        P("tp"),
        P("tp", None),
        P("tp", None),
        P("rows", "tp"),
        P("rows", "tp"),
    )
    out_specs = (P("rows", "tp"), P("rows", "tp"), P("rows", "tp"), P("rows", "tp"))
    return jax.shard_map(
        on_device, mesh=mesh, in_specs=in_specs, out_specs=out_specs, check_vma=False
    )
```
